32 devices in a mesh: section: 4 (over x, core), dp: 2 (over y), tensor: 4 (over z).
Axes of the slice: x: 2, y: 2, z: 4, core: 2. Of those that a mesh axis runs over, the one named last changes fastest.
Arguments:
- saved: bfloat16 [4, 1024, 5120], P('section', ('dp', 'tensor')), may hold values from -0.1875 to 0.1875
- weight: bfloat16 [4, 5120, 5120], P('section', None, 'tensor'), may hold values from -0.078125 to 0.078125
- out_grad: bfloat16 [1024, 5120], P(('dp', 'tensor')), may hold values from -6 to 6
Outputs:
- input_grads: bfloat16 [4, 1024, 5120], P('section', ('dp', 'tensor'))
- weight_grads: float32 [4, 5120, 5120], P('section', 'dp', 'tensor')
The draws below stay inside these ranges and needn't reach their ends.
All inputs are finite; a program needn't handle non-finite values.
Results may differ from the reference program's by a relative error of at most 0.02.
Values may be sent and summed in bfloat16 or wider, within the bound.
No kernel may reach another device: no remote copies, remote signals or barrier semaphores. Data moves between devices by JAX's collectives and lax.ppermute only.
A program may use at most 192 MiB of HBM per device.

```python
import jax
import jax.numpy as jnp
from jax import lax

D = 5120
SEQ = 512
TOKENS = 1024
N_SECTION = 4
N_DP = 2
N_TENSOR = 4


def levels(key, dims, split, least, largest):
    level, own = 1.0, jax.random.fold_in(key, 6)
    for axis_at, parts in split:
        steps = jnp.exp(jax.random.uniform(jax.random.fold_in(own, axis_at), (parts,), jnp.float32, least / len(split), largest / len(split)))
        level = level * jnp.repeat(steps, dims[axis_at] // parts).reshape([-1 if axis == axis_at else 1 for axis in range(len(dims))])
    return level


def gaussian(key, dims, scale, reach, split=(), kind=jnp.bfloat16):
    values = scale * jax.random.normal(key, dims, jnp.float32)
    if split:
        values = values * levels(key, dims, split, -0.22, 0.18)
    return jnp.clip(values, -reach, reach).astype(kind)


def setup_inputs(seed: int = 0) -> dict:
    arg_keys = jax.random.split(jax.random.key(seed), 4)
    saved = gaussian(arg_keys[0], (N_SECTION, TOKENS, D), (TOKENS ** -0.5), 0.1875, ((0, 4), (1, 8)))
    weight = gaussian(arg_keys[1], (N_SECTION, D, D), D ** -0.5, 0.078125, ((0, 4), (2, 4)))
    out_grad = gaussian(arg_keys[2], (TOKENS, D), 1.0, 6.0, ((0, 8),))
    return dict(saved=saved, weight=weight, out_grad=out_grad)


def reference(saved, weight, out_grad):
    width = D // N_TENSOR
    gradient = out_grad
    input_list = [None] * N_SECTION
    weight_list = [None] * N_SECTION
    for layer_section in reversed(range(N_SECTION)):
        matrix = weight[layer_section]
        total = jnp.zeros((TOKENS, D), jnp.float32)
        for column_block in range(N_TENSOR):
            grad_block = gradient[:, column_block * width:(column_block + 1) * width]
            weight_block = matrix[:, column_block * width:(column_block + 1) * width]
            partial_sum = jnp.dot(grad_block, weight_block.T, preferred_element_type=jnp.float32)
            partial_sum = lax.optimization_barrier(partial_sum.astype(jnp.bfloat16)).astype(jnp.float32)
            total = total + partial_sum
        updated = (gradient.astype(jnp.float32) + total).astype(jnp.bfloat16)
        summed = jnp.zeros((D, D), jnp.float32)
        for replica in range(N_DP):
            inputs_q = saved[layer_section, replica * SEQ:(replica + 1) * SEQ]
            grads_q = gradient[replica * SEQ:(replica + 1) * SEQ]
            seq_part = jnp.dot(inputs_q.T, grads_q, preferred_element_type=jnp.float32)
            seq_part = lax.optimization_barrier(seq_part.astype(jnp.bfloat16)).astype(jnp.float32)
            summed = summed + seq_part
        input_list[layer_section] = updated
        weight_list[layer_section] = summed
        gradient = updated
    return jnp.stack(input_list), jnp.stack(weight_list)
```

```python
import functools

import jax
import jax.numpy as jnp
from jax import lax
from jax.experimental import pallas as pl
from jax.experimental.pallas import tpu as pltpu
from jax.sharding import PartitionSpec as P

AXES = ("section", "dp", "tensor")
CHUNKS = 2
VMEM = 56 * 1024 * 1024
F32 = jnp.float32
BF16 = jnp.bfloat16
ANY = pl.BlockSpec(memory_space=pl.ANY)


def params(*semantics):
    return pltpu.CompilerParams(vmem_limit_bytes=VMEM, dimension_semantics=semantics or None)


def divisor(total, options):
    for option in options:
        if total % option == 0:
            return option
    return total


def product(lhs, rhs):
    return lax.dot_general(lhs, rhs, (((1,), (1,)), ((), ())), preferred_element_type=F32)


def send_kernel(count, active, where_ref, *refs):
    parts, weight_ref, grad_ref, out_ref = refs[:count], refs[count], refs[-2], refs[-1]

    @pl.when((pl.program_id(0) == 0) & (pl.program_id(1) == 0))
    def _():
        total = parts[0][...].astype(F32)
        for part in parts[1:]:
            total = total + part[...].astype(F32)
        grad_ref[...] = total.astype(BF16)

    @pl.when(where_ref[1] == active)
    def _():
        grad = grad_ref[...].reshape(-1, grad_ref.shape[-1])
        out_ref[0] = product(grad, weight_ref[0]).astype(BF16)

    @pl.when(where_ref[1] != active)
    def _():
        out_ref[...] = jnp.zeros_like(out_ref)


def send_products(active, where, parts, weights, after=()):
    shards, width, _ = weights.shape
    rows = parts[0].shape[-3:]
    tokens = rows[0] * rows[1]
    step = divisor(width, (640, 512, 256, 128))
    whole = pl.BlockSpec(rows, lambda g, j, w: (0, 0, 0))
    return pl.pallas_call(
        functools.partial(send_kernel, len(parts), active),
        grid_spec=pltpu.PrefetchScalarGridSpec(
            num_scalar_prefetch=1,
            grid=(shards // 2, width // step),
            in_specs=[whole] * len(parts)
            + [pl.BlockSpec((1, step, width), lambda g, j, w: ((w[0] ^ (2 * g + 1)) * (w[1] == active), j * (w[1] == active), 0))]
            + [ANY] * len(after),
            out_specs=[whole, pl.BlockSpec((1, tokens, step), lambda g, j, w: (g, 0, j))],
        ),
        out_shape=[
            jax.ShapeDtypeStruct(rows, BF16),
            jax.ShapeDtypeStruct((shards // 2, tokens, width), BF16),
        ],
        compiler_params=params("arbitrary", "arbitrary"),
        cost_estimate=pl.CostEstimate(
            flops=tokens * width * width * shards, bytes_accessed=width * width * shards, transcendentals=0
        ),
        name="send_products",
    )(where, *parts, weights, *after)


def keep_kernel(active, where_ref, grad_ref, weight_ref, *refs):
    out_ref = refs[-1]
    step = out_ref.shape[-1]

    @pl.when(where_ref[1] == active)
    def _():
        grad = grad_ref[...].reshape(-1, grad_ref.shape[-1])
        out_ref[0] = product(grad, weight_ref[0])

    @pl.when((where_ref[1] == active) & (pl.program_id(0) == 0))
    def _():
        columns = pl.ds(pl.multiple_of(pl.program_id(1) * step, 128), step)
        out_ref[0] += grad_ref[:, :, columns].reshape(-1, step).astype(F32)

    @pl.when(where_ref[1] != active)
    def _():
        out_ref[...] = jnp.zeros_like(out_ref)


def keep_products(active, where, grad, weights, after=()):
    shards, width, _ = weights.shape
    rows = grad.shape
    tokens = rows[0] * rows[1]
    step = divisor(width, (640, 512, 256, 128))
    return pl.pallas_call(
        functools.partial(keep_kernel, active),
        grid_spec=pltpu.PrefetchScalarGridSpec(
            num_scalar_prefetch=1,
            grid=(shards // 2, width // step),
            in_specs=[
                pl.BlockSpec(rows, lambda g, j, w: (0, 0, 0)),
                pl.BlockSpec((1, step, width), lambda g, j, w: ((w[0] ^ (2 * g)) * (w[1] == active), j * (w[1] == active), 0)),
            ]
            + [ANY] * len(after),
            out_specs=pl.BlockSpec((1, tokens, step), lambda g, j, w: (g, 0, j)),
        ),
        out_shape=jax.ShapeDtypeStruct((shards // 2, tokens, width), F32),
        compiler_params=params("arbitrary", "arbitrary"),
        cost_estimate=pl.CostEstimate(
            flops=tokens * width * width * shards, bytes_accessed=width * width * shards, transcendentals=0
        ),
        name="keep_products",
    )(where, grad, weights, *after)


def add_kernel(kept_ref, received_ref, *refs):
    own_ref, next_ref = refs[-2], refs[-1]
    own_ref[...] = (kept_ref[0] + received_ref[0].astype(F32)).astype(own_ref.dtype).reshape(own_ref.shape)
    next_ref[...] = (kept_ref[1] + received_ref[1].astype(F32)).astype(next_ref.dtype).reshape(next_ref.shape)


def add_received(kept, received, shape, own_dtype, after=()):
    return pl.pallas_call(
        add_kernel,
        in_specs=[pl.BlockSpec(memory_space=pltpu.VMEM)] * 2 + [ANY] * len(after),
        out_specs=[pl.BlockSpec(memory_space=pltpu.VMEM)] * 2,
        out_shape=[jax.ShapeDtypeStruct(shape, own_dtype), jax.ShapeDtypeStruct(shape, BF16)],
        compiler_params=params(),
        name="add_received",
    )(kept, received, *after)


def last_kernel(active, count, where_ref, own_ref, part_ref, weight_ref, *refs):
    grad_ref, send_ref, keep_ref, ordered = refs[count:]
    shards, rows, width = grad_ref.shape
    step = weight_ref.shape[1]
    n, j = pl.program_id(0), pl.program_id(1)

    @pl.when((n == 0) & (j == 0))
    def _():
        grad_ref[...] = (own_ref[...].astype(F32) + part_ref[...].astype(F32)).astype(BF16)
        for k in range(shards):
            ordered[k] = grad_ref[where_ref[0] ^ k]

    @pl.when(where_ref[1] == active)
    def _():
        columns = pl.ds(pl.multiple_of(j * step, 128), step)
        total = product(ordered[...].reshape(shards * rows, width), weight_ref[0])
        through = ordered[:, :, columns].reshape(shards * rows, step).astype(F32)
        total = total + jnp.where(n == where_ref[0], through, 0.0)
        total = total.reshape(shards // 2, 2, rows, step)
        keep_ref[...] = total[:, 0]
        send_ref[...] = total[:, 1].astype(BF16)

    @pl.when(where_ref[1] != active)
    def _():
        keep_ref[...] = jnp.zeros_like(keep_ref)
        send_ref[...] = jnp.zeros_like(send_ref)


def last_products(active, where, own, part, weights, after=()):
    shards, width, _ = weights.shape
    rows = own.shape[1]
    step = divisor(width, (640, 512, 256, 128))
    blocks = width // step
    whole = pl.BlockSpec(own.shape, lambda n, j, w: (0, 0, 0))
    halves = pl.BlockSpec((shards // 2, rows, step), lambda n, j, w: (0, 0, n * blocks + j))
    return pl.pallas_call(
        functools.partial(last_kernel, active, len(after)),
        grid_spec=pltpu.PrefetchScalarGridSpec(
            num_scalar_prefetch=1,
            grid=(shards, blocks),
            in_specs=[
                whole,
                whole,
                pl.BlockSpec((1, step, width), lambda n, j, w: (n * (w[1] == active), j * (w[1] == active), 0)),
            ]
            + [ANY] * len(after),
            out_specs=[whole, halves, halves],
            scratch_shapes=[pltpu.VMEM(own.shape, BF16)],
        ),
        out_shape=[
            jax.ShapeDtypeStruct(own.shape, BF16),
            jax.ShapeDtypeStruct((shards // 2, rows, shards * width), BF16),
            jax.ShapeDtypeStruct((shards // 2, rows, shards * width), F32),
        ],
        compiler_params=params("arbitrary", "arbitrary"),
        cost_estimate=pl.CostEstimate(
            flops=2 * shards * rows * width * width * shards,
            bytes_accessed=2 * width * width * shards,
            transcendentals=0,
        ),
        name="last_products",
    )(where, own, part, weights, *after)


def place_kernel(count, where_ref, *refs):
    pieces, outs = refs[:count], refs[count:]
    rows = outs[0].shape[1]
    for i, out_ref in enumerate(outs):
        for k, piece in enumerate(pieces):
            out_ref[where_ref[0] ^ k] = piece[i * rows:(i + 1) * rows]


def place_shards(where, pieces, chunks):
    tokens, width = pieces[0].shape
    memory = pl.BlockSpec(memory_space=pltpu.VMEM)
    return pl.pallas_call(
        functools.partial(place_kernel, len(pieces)),
        in_specs=[pl.BlockSpec(memory_space=pltpu.SMEM)] + [memory] * len(pieces),
        out_specs=[memory] * chunks,
        out_shape=[jax.ShapeDtypeStruct((len(pieces), tokens // chunks, width), BF16)] * chunks,
        compiler_params=params(),
        name="place_shards",
    )(where, *pieces)


def inputs_kernel(shards, chunks, where_ref, *refs):
    pieces, owns, parts, out_ref = refs[:shards], refs[shards:shards + chunks], refs[shards + chunks:-1], refs[-1]
    width = pieces[0].shape[-1]
    rows = owns[0].shape[0]
    for i in range(chunks):
        out_ref[i * rows:(i + 1) * rows] = (owns[i][...] + parts[i][...].astype(F32)).astype(BF16)
    for k in range(shards):
        columns = pl.ds(pl.multiple_of((where_ref[0] ^ k) * width, 128), width)
        out_ref[:, columns] = out_ref[:, columns] + pieces[k][...]


def place_inputs(where, pieces, owns, parts):
    memory = pl.BlockSpec(memory_space=pltpu.VMEM)
    return pl.pallas_call(
        functools.partial(inputs_kernel, len(pieces), len(owns)),
        in_specs=[pl.BlockSpec(memory_space=pltpu.SMEM)] + [memory] * (len(pieces) + 2 * len(owns)),
        out_specs=memory,
        out_shape=jax.ShapeDtypeStruct((pieces[0].shape[0], pieces[0].shape[1] * len(pieces)), BF16),
        compiler_params=params(),
        name="place_inputs",
    )(where, *pieces, *owns, *parts)


def weight_kernel(shards, replicas, where_ref, *refs):
    saved, grads, out_ref, ordered = refs[:shards], refs[shards:shards + replicas], refs[-2], refs[-1]
    _, _, rows, width = grads[0].shape
    tokens = saved[0].shape[0] // replicas

    @pl.when(pl.program_id(0) == 0)
    def _():
        for k in range(shards):
            for j, grad in enumerate(grads):
                at = (k * replicas + j) * tokens
                ordered[at:at + tokens] = grad[:, where_ref[0] ^ k].reshape(tokens, width)

    total = None
    for k in range(shards):
        part = lax.dot_general(
            saved[k][...],
            ordered[k * replicas * tokens:(k + 1) * replicas * tokens],
            (((0,), (0,)), ((), ())),
            preferred_element_type=F32,
        )
        total = part if total is None else total + part
    out_ref[...] = total


def weight_products(where, saved, grads, after=()):
    tokens, features = saved[0].shape
    width = grads[0].shape[-1]
    step = divisor(features, (256, 128))
    whole = pl.BlockSpec(grads[0].shape, lambda n, w: (0, 0, 0, 0))
    shards = len(saved)
    return pl.pallas_call(
        functools.partial(weight_kernel, shards, len(grads)),
        grid_spec=pltpu.PrefetchScalarGridSpec(
            num_scalar_prefetch=1,
            grid=(features // step,),
            in_specs=[pl.BlockSpec((tokens, step), lambda n, w: (0, n))] * shards
            + [whole] * len(grads)
            + [ANY] * len(after),
            out_specs=pl.BlockSpec((step, width), lambda n, w: (n, 0)),
            scratch_shapes=[pltpu.VMEM((shards * tokens, width), BF16)],
        ),
        out_shape=jax.ShapeDtypeStruct((features, width), F32),
        compiler_params=params("arbitrary"),
        cost_estimate=pl.CostEstimate(
            flops=2 * shards * tokens * features * width,
            bytes_accessed=4 * features * width + 2 * shards * tokens * features,
            transcendentals=0,
        ),
        name="weight_products",
    )(where, *saved, *grads, *after)


def on_device(sections, replicas, shards, saved, weight, out_grad):
    tokens, model = out_grad.shape
    width = model // shards
    chunks = CHUNKS
    rows = tokens // chunks
    section, dp, tensor = (lax.axis_index(a) for a in AXES)
    weights = weight[0].reshape(shards, width, width)
    activations = saved[0]

    def place(s, d, t):
        return (s * replicas + d) * shards + t

    def permute(value, route, active):
        pairs = []
        for s in active:
            for d in range(replicas):
                for t in range(shards):
                    to = route(s, d, t)
                    if 0 <= to[0] < sections:
                        pairs.append((place(s, d, t), place(*to)))
        return lax.ppermute(value, AXES, pairs)

    def across(k):
        return lambda s, d, t: (s, d, t ^ k)

    everyone = range(sections)
    where = jnp.stack([tensor, section]).astype(jnp.int32)

    last = sections - 1
    pieces = [lax.dynamic_slice(out_grad, (0, tensor * width), (tokens, width)) * (section == last).astype(BF16)]
    for k in range(1, shards):
        block = lax.dynamic_slice(out_grad, (0, (tensor ^ k) * width), (tokens, width))
        pieces.append(permute(block, across(k), [last]))
    first = place_shards(where, pieces, chunks)

    height = model // replicas
    own_rows = [lax.dynamic_slice(activations, (0, dp * height), (tokens, height))]
    for j in range(1, replicas):
        block = lax.dynamic_slice(activations, (0, lax.rem(dp + replicas - j, replicas) * height), (tokens, height))
        own_rows.append(
            permute(block, lambda s, d, t: (s, (d - j) % replicas, t), everyone)
        )
    own_rows = jnp.concatenate(own_rows, axis=0)
    far = permute(own_rows, across(2), everyone)
    near = permute(own_rows, across(1), everyone), permute(far, across(1), everyone)
    gathered = [own_rows, near[0], far, near[1]]
    waits = {1: (own_rows,), 2: (far,), 3: near}

    kept = []
    incoming = [(first[i],) for i in range(chunks)]
    for r in range(sections):
        active = sections - 1 - r
        grads, outgoing = [], []
        for i in range(chunks):
            after = waits.get(r, ()) if i == 0 else ()
            if active > 0:
                grad, send = send_products(active, where, incoming[i], weights, after)
                received = permute(send, across(1), [active])
                keep = keep_products(active, where, grad, weights)
                own, part = add_received(keep, received, grad.shape, BF16)
                down = permute(own, lambda s, d, t: (s - 1, d, t), [active])
                outgoing.append((down, permute(part, lambda s, d, t: (s - 1, d, t ^ 2), [active])))
            else:
                grad, send, keep = last_products(active, where, *incoming[i], weights, after)
                received = permute(send, across(1), [active])
                own, part = add_received(keep, received, (rows, model), F32)
                outgoing.append((own, permute(part, across(2), [active])))
            grads.append(grad)
        incoming = outgoing
        kept.append(grads)

    mine = jnp.stack([functools.reduce(jnp.add, [grads[i] for grads in kept]) for i in range(chunks)])
    others = [
        permute(mine, lambda s, d, t: (s, (d - j) % replicas, t), everyone) for j in range(1, replicas)
    ]

    back = []
    for k in range(shards):
        block = lax.dynamic_slice(mine, (0, tensor ^ k, 0, 0), (chunks, 1, rows, width)).reshape(tokens, width)
        back.append(permute(block, lambda s, d, t: (s + 1, d, t ^ k), range(sections - 1)))
    weight_grad = weight_products(where, gathered, [mine] + others)
    own_input = place_inputs(where, back, [pair[0] for pair in incoming], [pair[1] for pair in incoming])
    return (own_input[None], weight_grad[None])


def solution(mesh):
    placed = (
        P("section", ("dp", "tensor"), None),
        P("section", None, "tensor"),
        P(("dp", "tensor"), None),
    )
    sizes = [mesh.shape[a] for a in AXES]
    return jax.shard_map(
        functools.partial(on_device, *sizes),
        mesh=mesh,
        in_specs=placed,
        out_specs=(P("section", ("dp", "tensor"), None), P("section", "dp", "tensor")),
        check_vma=False,
    )
```

```python
import functools

import jax
import jax.numpy as jnp
from jax import lax
from jax.experimental import pallas as pl
from jax.experimental.pallas import tpu as pltpu
from jax.sharding import PartitionSpec as P

AXES = ("section", "dp", "tensor")
CHUNKS = 2
STEP = 1280
PIECES = 1
VMEM = 56 * 1024 * 1024
ADD = 52 * 1024 * 1024
SMALL = 48 * 1024 * 1024
F32 = jnp.float32
BF16 = jnp.bfloat16
LONG = pl.CostEstimate(flops=200000000000, bytes_accessed=1000, transcendentals=0)
BRIEF = pl.CostEstimate(flops=1000, bytes_accessed=1000, transcendentals=0)
ANY = pl.BlockSpec(memory_space=pl.ANY)


def params(limit=VMEM):
    return pltpu.CompilerParams(vmem_limit_bytes=limit)


def divisor(total, options):
    for option in options:
        if total % option == 0:
            return option
    return total


def product(lhs, rhs):
    return lax.dot_general(lhs, rhs, (((1,), (1,)), ((), ())), preferred_element_type=F32)


def products_kernel(active, order, count, after, formed, step, where_ref, *refs):
    parts, weight_ref, outs = refs[:count], refs[count], refs[count + 1 + after:-6]
    part_mem, grad_mem, weight_mem, out_mem, load_sem, store_sem = refs[-6:]
    rows, width = grad_mem.shape[0] * grad_mem.shape[1], grad_mem.shape[2]
    steps = width // step

    @pl.when(where_ref[1] == active)
    def _():
        part_loads = [
            pltpu.make_async_copy(part, part_mem.at[p], load_sem.at[p]) for p, part in enumerate(parts)
        ]
        height = step // PIECES
        weight_loads = [
            pltpu.make_async_copy(
                weight_ref.at[where_ref[0] ^ k, pl.ds(c * height, height)],
                weight_mem.at[b, pl.ds(c * height, height)],
                load_sem.at[count + b * steps * PIECES + c],
            )
            for b, k in enumerate(order)
            for c in range(steps * PIECES)
        ]
        for load in part_loads + weight_loads:
            load.start()
        for load in part_loads:
            load.wait()
        if formed:
            total = part_mem[0].astype(F32)
            for p in range(1, count):
                total = total + part_mem[p].astype(F32)
            grad_mem[...] = total.astype(BF16)
            source = grad_mem
        else:
            source = part_mem.at[0]
        stores = []
        if formed:
            stores.append(pltpu.make_async_copy(grad_mem, outs[0], store_sem.at[0]))
            stores[0].start()
        for b, k in enumerate(order):
            for c in range(steps):
                for load in weight_loads[(b * steps + c) * PIECES:(b * steps + c + 1) * PIECES]:
                    load.wait()
                total = product(source[...].reshape(rows, width), weight_mem[b, c * step:(c + 1) * step])
                if k == 0:
                    total = total + source[:, :, c * step:(c + 1) * step].reshape(rows, step).astype(F32)
                out_mem[b, :, c * step:(c + 1) * step] = total.astype(BF16)
            stores.append(pltpu.make_async_copy(out_mem.at[b], outs[len(stores)], store_sem.at[len(stores)]))
            stores[-1].start()
        for store in stores:
            store.wait()


def products(active, where, parts, weights, order, formed, name, cost, after=()):
    shards, width, _ = weights.shape
    shape = parts[0].shape
    tokens = shape[0] * shape[1]
    step = divisor(width, (STEP, 256, 128))
    loads = len(parts) + len(order) * (width // step) * PIECES
    block = jax.ShapeDtypeStruct((tokens, width), BF16)
    return pl.pallas_call(
        functools.partial(products_kernel, active, order, len(parts), len(after), formed, step),
        in_specs=[pl.BlockSpec(memory_space=pltpu.SMEM)] + [ANY] * (len(parts) + 1 + len(after)),
        out_specs=[ANY] * (len(order) + formed),
        out_shape=[jax.ShapeDtypeStruct(shape, BF16)] * formed + [block] * len(order),
        scratch_shapes=[
            pltpu.VMEM((len(parts), *shape), BF16),
            pltpu.VMEM(shape, BF16),
            pltpu.VMEM((len(order), width, width), BF16),
            pltpu.VMEM((len(order), tokens, width), BF16),
            pltpu.SemaphoreType.DMA((loads,)),
            pltpu.SemaphoreType.DMA((len(order) + formed,)),
        ],
        compiler_params=params(),
        cost_estimate=cost,
        name=name,
    )(where, *parts, weights, *after)


def lead_products(active, where, parts, weights, after=()):
    return products(active, where, parts, weights, (3,), 1, "lead_products", BRIEF, after)


def rest_products(active, where, grad, weights, after=()):
    return products(active, where, (grad,), weights, (2, 1, 0), 0, "rest_products", LONG, after)


def add_kernel(active, where_ref, kept_ref, received_ref, *refs):
    out_ref, kept, received, total, sem = refs[-5:]

    @pl.when(where_ref[1] == active)
    def _():
        loads = [
            pltpu.make_async_copy(kept_ref, kept, sem.at[0]),
            pltpu.make_async_copy(received_ref, received, sem.at[1]),
        ]
        for load in loads:
            load.start()
        for load in loads:
            load.wait()
        total[...] = (kept[...].astype(F32) + received[...].astype(F32)).astype(BF16)
        store = pltpu.make_async_copy(total, out_ref, sem.at[2])
        store.start()
        store.wait()


def add_received(active, where, kept, received, after=()):
    return pl.pallas_call(
        functools.partial(add_kernel, active),
        in_specs=[pl.BlockSpec(memory_space=pltpu.SMEM)] + [ANY] * (2 + len(after)),
        out_specs=ANY,
        out_shape=jax.ShapeDtypeStruct(received.shape, BF16),
        scratch_shapes=[pltpu.VMEM(received.shape, BF16)] * 3 + [pltpu.SemaphoreType.DMA((3,))],
        compiler_params=params(ADD),
        cost_estimate=BRIEF,
        name="add_received",
    )(where, kept, received, *after)


def last_kernel(active, count, after, step, where_ref, *refs):
    parts, weight_ref, outs = refs[:count], refs[count], refs[count + 1 + after:-7]
    part_mem, grad_mem, weight_mem, out_mem, own_mem, load_sem, store_sem = refs[-7:]
    shards, rows, width = grad_mem.shape
    steps = width // step

    @pl.when(where_ref[1] == active)
    def _():
        part_loads = [
            pltpu.make_async_copy(part, part_mem.at[p], load_sem.at[p]) for p, part in enumerate(parts)
        ]
        height = step // PIECES
        weight_loads = [
            pltpu.make_async_copy(
                weight_ref.at[n, pl.ds(c * height, height)],
                weight_mem.at[n, pl.ds(c * height, height)],
                load_sem.at[count + n * steps * PIECES + c],
            )
            for n in range(shards)
            for c in range(steps * PIECES)
        ]
        for load in part_loads + weight_loads:
            load.start()
        for load in part_loads:
            load.wait()
        total = part_mem[0].astype(F32)
        for p in range(1, count):
            total = total + part_mem[p].astype(F32)
        part_mem[0] = total.astype(BF16)
        stores = [pltpu.make_async_copy(part_mem.at[0], outs[0], store_sem.at[0])]
        stores[0].start()
        for k in range(shards):
            grad_mem[k] = part_mem[0, where_ref[0] ^ k]
        for n in range(shards):
            for c in range(steps):
                for load in weight_loads[(n * steps + c) * PIECES:(n * steps + c + 1) * PIECES]:
                    load.wait()
                at = slice(n * width + c * step, n * width + (c + 1) * step)
                total = product(grad_mem[...].reshape(shards * rows, width), weight_mem[n, c * step:(c + 1) * step])
                through = grad_mem[:, :, c * step:(c + 1) * step].reshape(shards * rows, step).astype(F32)
                total = total + jnp.where(where_ref[0] == n, through, 0.0)
                own_mem[:, at] = total[:rows]
                for k in range(1, shards):
                    out_mem[k - 1, :, at] = total[k * rows:(k + 1) * rows].astype(BF16)
        for k in range(1, shards):
            stores.append(pltpu.make_async_copy(out_mem.at[k - 1], outs[k], store_sem.at[k]))
        stores.append(pltpu.make_async_copy(own_mem, outs[shards], store_sem.at[shards]))
        for store in stores[1:]:
            store.start()
        for store in stores:
            store.wait()


def last_products(active, where, parts, weights, after=()):
    shards, width, _ = weights.shape
    shape = parts[0].shape
    rows = shape[1]
    step = divisor(width, (STEP, 256, 128))
    half = jax.ShapeDtypeStruct((rows, shards * width), BF16)
    return pl.pallas_call(
        functools.partial(last_kernel, active, len(parts), len(after), step),
        in_specs=[pl.BlockSpec(memory_space=pltpu.SMEM)] + [ANY] * (len(parts) + 1 + len(after)),
        out_specs=[ANY] * (shards + 1),
        out_shape=[jax.ShapeDtypeStruct(shape, BF16)]
        + [half] * (shards - 1)
        + [jax.ShapeDtypeStruct((rows, shards * width), F32)],
        scratch_shapes=[
            pltpu.VMEM((len(parts), *shape), BF16),
            pltpu.VMEM(shape, BF16),
            pltpu.VMEM(weights.shape, BF16),
            pltpu.VMEM((shards - 1, rows, shards * width), BF16),
            pltpu.VMEM((rows, shards * width), F32),
            pltpu.SemaphoreType.DMA((len(parts) + shards * (width // step) * PIECES,)),
            pltpu.SemaphoreType.DMA((shards + 1,)),
        ],
        compiler_params=params(),
        cost_estimate=BRIEF,
        name="last_products",
    )(where, *parts, weights, *after)


def place_kernel(count, where_ref, *refs):
    pieces, outs = refs[:count], refs[count:]
    rows = outs[0].shape[1]
    for i, out_ref in enumerate(outs):
        for k, piece in enumerate(pieces):
            out_ref[where_ref[0] ^ k] = piece[i * rows:(i + 1) * rows]


def place_shards(where, pieces, chunks):
    tokens, width = pieces[0].shape
    memory = pl.BlockSpec(memory_space=pltpu.VMEM)
    return pl.pallas_call(
        functools.partial(place_kernel, len(pieces)),
        in_specs=[pl.BlockSpec(memory_space=pltpu.SMEM)] + [memory] * len(pieces),
        out_specs=[memory] * chunks,
        out_shape=[jax.ShapeDtypeStruct((len(pieces), tokens // chunks, width), BF16)] * chunks,
        compiler_params=params(SMALL),
        name="place_shards",
    )(where, *pieces)


def first_kernel(where_ref, *refs):
    out_ref = refs[-1]
    for i in range((len(refs) - 2) // 3):
        own, near, far = refs[3 * i:3 * i + 3]
        rows = own.shape[0]
        total = (own[...] + near[...].astype(F32) + far[...].astype(F32)).astype(BF16)
        out_ref[i * rows:(i + 1) * rows] = jnp.where(where_ref[1] == 0, total, jnp.zeros_like(total))


def first_inputs(where, sums, tokens, model, after):
    memory = pl.BlockSpec(memory_space=pltpu.VMEM)
    terms = [term for chunk in sums for term in chunk]
    return pl.pallas_call(
        first_kernel,
        in_specs=[pl.BlockSpec(memory_space=pltpu.SMEM)] + [memory] * len(terms) + [ANY],
        out_specs=memory,
        out_shape=jax.ShapeDtypeStruct((tokens, model), BF16),
        compiler_params=params(SMALL),
        cost_estimate=BRIEF,
        name="first_inputs",
    )(where, *terms, after)


def inputs_kernel(where_ref, sums_ref, *refs):
    pieces, out_ref = refs[:-1], refs[-1]
    width = pieces[0].shape[-1]
    for k, piece in enumerate(pieces):
        columns = pl.ds(pl.multiple_of((where_ref[0] ^ k) * width, 128), width)
        out_ref[:, columns] = sums_ref[:, columns] + piece[...]


def place_inputs(where, sums, pieces):
    memory = pl.BlockSpec(memory_space=pltpu.VMEM)
    return pl.pallas_call(
        inputs_kernel,
        in_specs=[pl.BlockSpec(memory_space=pltpu.SMEM)] + [memory] * (1 + len(pieces)),
        out_specs=memory,
        out_shape=jax.ShapeDtypeStruct(sums.shape, BF16),
        compiler_params=params(SMALL),
        name="place_inputs",
    )(where, sums, *pieces)


def cut_kernel(owners, chunks, where_ref, *refs):
    held, sem = refs[-2:]
    shards = held.shape[0]
    outs = refs[-2 - shards:-2]
    rows = refs[0].shape[1]
    for o, section in enumerate(owners):
        grads = refs[o * chunks:(o + 1) * chunks]

        @pl.when(where_ref[1] == section)
        def _():
            loads = [
                pltpu.make_async_copy(grad.at[where_ref[0] ^ k], held.at[k, pl.ds(i * rows, rows)], sem.at[k, i])
                for k in range(shards)
                for i, grad in enumerate(grads)
            ]
            for load in loads:
                load.start()
            for load in loads:
                load.wait()
            stores = [pltpu.make_async_copy(held.at[k], out, sem.at[k, 0]) for k, out in enumerate(outs)]
            for store in stores:
                store.start()
            for store in stores:
                store.wait()


def cut_shards(where, owners, after):
    grads = [grad for _, chunk in owners for grad in chunk]
    chunks = len(owners[0][1])
    shards, rows, width = grads[0].shape
    tokens = rows * chunks
    return pl.pallas_call(
        functools.partial(cut_kernel, [section for section, _ in owners], chunks),
        in_specs=[pl.BlockSpec(memory_space=pltpu.SMEM)] + [ANY] * (len(grads) + len(after)),
        out_specs=[ANY] * shards,
        out_shape=[jax.ShapeDtypeStruct((tokens, width), BF16)] * shards,
        scratch_shapes=[
            pltpu.VMEM((shards, tokens, width), BF16),
            pltpu.SemaphoreType.DMA((shards, chunks)),
        ],
        compiler_params=params(SMALL),
        cost_estimate=BRIEF,
        name="cut_shards",
    )(where, *grads, *after)


def pick_kernel(owners, chunks, where_ref, *refs):
    out_ref, held, sem = refs[-3:]
    for o, section in enumerate(owners):
        grads = refs[o * chunks:(o + 1) * chunks]

        @pl.when(where_ref[1] == section)
        def _():
            loads = [pltpu.make_async_copy(grad, held.at[i], sem.at[i]) for i, grad in enumerate(grads)]
            for load in loads:
                load.start()
            for load in loads:
                load.wait()
            store = pltpu.make_async_copy(held, out_ref, sem.at[0])
            store.start()
            store.wait()


def pick(where, owners, after):
    grads = [grad for _, chunk in owners for grad in chunk]
    shape = (len(owners[0][1]), *grads[0].shape)
    return pl.pallas_call(
        functools.partial(pick_kernel, [section for section, _ in owners], shape[0]),
        in_specs=[pl.BlockSpec(memory_space=pltpu.SMEM)] + [ANY] * (len(grads) + len(after)),
        out_specs=ANY,
        out_shape=jax.ShapeDtypeStruct(shape, BF16),
        scratch_shapes=[pltpu.VMEM(shape, BF16), pltpu.SemaphoreType.DMA(shape[:1])],
        compiler_params=params(SMALL),
        cost_estimate=BRIEF,
        name="pick",
    )(where, *grads, *after)


def mark_kernel(*refs):
    refs[-1][...] = jnp.zeros_like(refs[-1])


def mark(cost, *after):
    return pl.pallas_call(
        mark_kernel,
        in_specs=[ANY] * len(after),
        out_specs=pl.BlockSpec(memory_space=pltpu.VMEM),
        out_shape=jax.ShapeDtypeStruct((8, 128), F32),
        compiler_params=params(SMALL),
        cost_estimate=cost,
        name="mark",
    )(*after)


def join_kernel(sections, count, where_ref, *refs):
    parts, out_ref, held, sem = refs[:count], refs[-3], refs[-2], refs[-1]
    rows = parts[0].shape[0]

    @pl.when((where_ref[1] >= sections[0]) & (where_ref[1] <= sections[-1]))
    def _():
        loads = [
            pltpu.make_async_copy(part, held.at[pl.ds(j * rows, rows)], sem.at[j]) for j, part in enumerate(parts)
        ]
        for load in loads:
            load.start()
        for load in loads:
            load.wait()
        store = pltpu.make_async_copy(held, out_ref, sem.at[0])
        store.start()
        store.wait()


def join(sections, where, parts, after):
    rows, width = parts[0].shape
    return pl.pallas_call(
        functools.partial(join_kernel, sections, len(parts)),
        in_specs=[pl.BlockSpec(memory_space=pltpu.SMEM)] + [ANY] * (len(parts) + 1),
        out_specs=ANY,
        out_shape=jax.ShapeDtypeStruct((rows * len(parts), width), BF16),
        scratch_shapes=[pltpu.VMEM((rows * len(parts), width), BF16), pltpu.SemaphoreType.DMA((len(parts),))],
        compiler_params=params(SMALL),
        cost_estimate=BRIEF,
        name="join",
    )(where, *parts, after)


def weight_kernel(owners, sections, shards, replicas, where_ref, *refs):
    groups, grads = refs[:len(owners) * shards], refs[len(owners) * shards:-6]
    out_ref, saved, ordered, out_mem, load_sem, store_sem = refs[-6:]
    chunks = (len(grads) - replicas + 1) // (sections + replicas - 1)
    _, rows, width = grads[0].shape
    tokens = chunks * rows
    step = out_mem.shape[1]
    steps = out_ref.shape[0] // step

    loads = []
    for k in range(shards):
        for g, owner in enumerate(owners):
            @pl.when((where_ref[1] >= owner[0]) & (where_ref[1] <= owner[-1]))
            def _():
                pltpu.make_async_copy(groups[g * shards + k], saved.at[k], load_sem.at[k]).start()

        loads.append(pltpu.make_async_copy(groups[k], saved.at[k], load_sem.at[k]))
    def grad_loads(section):
        for k in range(shards):
            for j in range(replicas):
                for i in range(chunks):
                    if j == 0:
                        grad = grads[section * chunks + i]
                    elif section == 0:
                        grad = grads[(sections + j - 1) * chunks + i]
                    else:
                        grad = grads[(sections + replicas - 1) * chunks + j - 1].at[i]
                    at = (k * replicas + j) * tokens + i * rows
                    yield pltpu.make_async_copy(
                        grad.at[where_ref[0] ^ k],
                        ordered.at[pl.ds(at, rows)],
                        load_sem.at[shards + (k * replicas + j) * chunks + i],
                    )

    for section in range(sections):
        @pl.when(where_ref[1] == section)
        def _():
            for load in grad_loads(section):
                load.start()

    loads.extend(grad_loads(0))
    for load in loads:
        load.wait()

    def store(n):
        slot = lax.rem(n, 2)
        return pltpu.make_async_copy(
            out_mem.at[slot], out_ref.at[pl.ds(pl.multiple_of(n * step, step), step)], store_sem.at[slot]
        )

    @pl.loop(0, steps)
    def _(n):
        @pl.when(n >= 2)
        def _():
            store(n - 2).wait()

        features = pl.ds(pl.multiple_of(n * step, step), step)
        out_mem[lax.rem(n, 2)] = lax.dot_general(
            saved[:, :, features].reshape(ordered.shape[0], step),
            ordered[...],
            (((0,), (0,)), ((), ())),
            preferred_element_type=F32,
        )
        store(n).start()

    for n in range(max(steps - 2, 0), steps):
        store(n).wait()


def weight_products(where, gathered, own_grads, first_peers, other_peers):
    owners = tuple(tuple(sections) for sections, _ in gathered)
    groups = [array for _, arrays in gathered for array in arrays]
    shards = len(gathered[0][1])
    tokens, features = groups[0].shape
    sections, replicas = len(own_grads), len(first_peers) + 1
    chunks, width = len(own_grads[0]), own_grads[0][0].shape[-1]
    grads = [grad for chunk in (*own_grads, *first_peers) for grad in chunk] + other_peers
    step = divisor(features, (256, 128))
    return pl.pallas_call(
        functools.partial(weight_kernel, owners, sections, shards, replicas),
        in_specs=[pl.BlockSpec(memory_space=pltpu.SMEM)] + [ANY] * (len(groups) + len(grads)),
        out_specs=ANY,
        out_shape=jax.ShapeDtypeStruct((features, width), F32),
        scratch_shapes=[
            pltpu.VMEM((shards, tokens, features), BF16),
            pltpu.VMEM((shards * tokens, width), BF16),
            pltpu.VMEM((2, step, width), F32),
            pltpu.SemaphoreType.DMA((shards + shards * replicas * chunks,)),
            pltpu.SemaphoreType.DMA((2,)),
        ],
        compiler_params=params(),
        cost_estimate=LONG,
        name="weight_products",
    )(where, *groups, *grads)


def on_device(sections, replicas, shards, saved, weight, out_grad):
    tokens, model = out_grad.shape
    width = model // shards
    chunks = CHUNKS
    rows = tokens // chunks
    section, dp, tensor = (lax.axis_index(a) for a in AXES)
    weights = weight[0].reshape(shards, width, width)
    activations = saved[0]

    def place(s, d, t):
        return (s * replicas + d) * shards + t

    def permute(value, route, active):
        pairs = []
        for s in active:
            for d in range(replicas):
                for t in range(shards):
                    to = route(s, d, t)
                    if 0 <= to[0] < sections:
                        pairs.append((place(s, d, t), place(*to)))
        return lax.ppermute(value, AXES, pairs)

    def across(k):
        return lambda s, d, t: (s, d, t ^ k)

    everyone = range(sections)
    where = jnp.stack([tensor, section]).astype(jnp.int32)

    last = sections - 1
    pieces = [lax.dynamic_slice(out_grad, (0, tensor * width), (tokens, width))]
    for k in range(1, shards):
        block = lax.dynamic_slice(out_grad, (0, (tensor ^ k) * width), (tokens, width))
        pieces.append(permute(block, across(k), [last]))
    first = place_shards(where, pieces, chunks)

    height = model // replicas
    own_rows = [lax.dynamic_slice(activations, (0, dp * height), (tokens, height))]
    for j in range(1, replicas):
        block = lax.dynamic_slice(activations, (0, lax.rem(dp + replicas - j, replicas) * height), (tokens, height))
        own_rows.append(
            permute(block, lambda s, d, t: (s, (d - j) % replicas, t), everyone)
        )

    def swap(value, active):
        return [permute(value, lambda s, d, t: (s, (d - j) % replicas, t), active) for j in range(1, replicas)]

    half = sections // 2
    low, high = range(half), range(half, sections)
    def gather(value, active):
        near, far = permute(value, across(1), active), permute(value, across(2), active)
        return [value, near, far, permute(far, across(1), active)]

    gathered, kept = [(low, gather(join(low, where, own_rows, first[0]), low))], []
    swapped = []
    due = {(0, 1): gathered[0][1][1:3], (half, 0): gathered[0][1][3:]}
    incoming = [(first[i],) for i in range(chunks)]
    ended = ()
    for r in range(sections - 1):
        active = sections - 1 - r
        grads, outgoing = [], []
        for i in range(chunks):
            before = outgoing[-1] if i else incoming[-1] if r else ()
            pinned = (*before[:2], *due.get((r, i), ()))
            grad, lead = lead_products(active, where, incoming[i], weights, ended)
            received = permute(lead, across(1), [active])
            if active == half - 1 and i == chunks - 1:
                token = permute(mark(BRIEF, grad), lambda s, d, t: (s + 1, d, t), range(half - 1, sections - 1))
                gathered.append((high, gather(join(high, where, own_rows, token), high)))
                pinned = (*pinned, token)
            keep, near, own = rest_products(active, where, grad, weights, pinned)
            sums = [
                permute(own.reshape(grad.shape), lambda s, d, t: (s - 1, d, t), [active]),
                permute(near.reshape(grad.shape), lambda s, d, t: (s - 1, d, t ^ 1), [active]),
            ]
            stop = (mark(LONG, keep, before[2]),) if i else (near,)
            part = add_received(active, where, keep, received, stop)
            sums.append(permute(part.reshape(grad.shape), lambda s, d, t: (s - 1, d, t ^ 2), [active]))
            ended = (part,)
            outgoing.append(sums)
            grads.append(grad)
        incoming = outgoing
        kept.append(grads)

    def send_back(owners, after):
        blocks = cut_shards(where, [(s, kept[sections - 1 - s]) for s in owners], after)
        return [permute(block, lambda s, d, t: (s + 1, d, t ^ k), owners) for k, block in enumerate(blocks)]

    first_products, finals, last_grads = [], [], []
    ended = (*ended, *gathered[-1][1][1:3])
    for i in range(chunks):
        grad, near, keep, lead, own = last_products(0, where, incoming[i], weights, ended)
        first_products.append((keep, permute(lead, across(1), [0])))
        finals.append([own, permute(near, across(1), [0])])
        swapped.append(swap(grad, [0]))
        if not i:
            picked = pick(where, [(s, kept[sections - 1 - s]) for s in range(1, sections)], (grad,))
            others = swap(picked, range(1, sections))
            ended = (mark(LONG, keep, *incoming[-1]),)
        last_grads.append(grad)
    kept.append(last_grads)
    ended = (keep,)
    for i, (keep, received) in enumerate(first_products):
        if i:
            ended = (mark(LONG, *ended, received, *swapped[0], *others),)
        part = add_received(0, where, keep, received, ended)
        finals[i].append(permute(part, across(2), [0]))
        ended = (part,)

    back = send_back(range(sections - 1), (part,))
    weight_grad = weight_products(where, gathered, kept[::-1], list(zip(*swapped)), others)
    own_input = place_inputs(where, first_inputs(where, finals, tokens, model, weight_grad), back)
    return (own_input[None], weight_grad[None])


def solution(mesh):
    placed = (
        P("section", ("dp", "tensor"), None),
        P("section", None, "tensor"),
        P(("dp", "tensor"), None),
    )
    sizes = [mesh.shape[a] for a in AXES]
    return jax.shard_map(
        functools.partial(on_device, *sizes),
        mesh=mesh,
        in_specs=placed,
        out_specs=(P("section", ("dp", "tensor"), None), P("section", "dp", "tensor")),
        check_vma=False,
    )
```

```python
import functools

import jax
import jax.numpy as jnp
from jax import lax
from jax.experimental import pallas as pl
from jax.experimental.pallas import tpu as pltpu
from jax.sharding import PartitionSpec as P

AXES = ("section", "dp", "tensor")
CHUNKS = 2
VMEM = 56 * 1024 * 1024
ADD = 52 * 1024 * 1024
SMALL = 48 * 1024 * 1024
F32 = jnp.float32
BF16 = jnp.bfloat16
LONG = pl.CostEstimate(flops=200000000000, bytes_accessed=1000, transcendentals=0)
BRIEF = pl.CostEstimate(flops=1000, bytes_accessed=1000, transcendentals=0)
ANY = pl.BlockSpec(memory_space=pl.ANY)


def params(limit=VMEM):
    return pltpu.CompilerParams(vmem_limit_bytes=limit)


def divisor(total, options):
    for option in options:
        if total % option == 0:
            return option
    return total


def product(lhs, rhs):
    return lax.dot_general(lhs, rhs, (((1,), (1,)), ((), ())), preferred_element_type=F32)


def products_kernel(active, order, count, after, formed, where_ref, *refs):
    parts, weight_ref, outs = refs[:count], refs[count], refs[count + 1 + after:-6]
    part_mem, grad_mem, weight_mem, out_mem, load_sem, store_sem = refs[-6:]
    rows, width = grad_mem.shape[0] * grad_mem.shape[1], grad_mem.shape[2]

    @pl.when(where_ref[1] == active)
    def _():
        part_loads = [
            pltpu.make_async_copy(part, part_mem.at[p], load_sem.at[p]) for p, part in enumerate(parts)
        ]
        weight_loads = [
            pltpu.make_async_copy(weight_ref.at[where_ref[0] ^ k], weight_mem.at[b], load_sem.at[count + b])
            for b, k in enumerate(order)
        ]
        for load in part_loads + weight_loads:
            load.start()
        for load in part_loads:
            load.wait()
        if formed:
            total = part_mem[0].astype(F32)
            for p in range(1, count):
                total = total + part_mem[p].astype(F32)
            grad_mem[...] = total.astype(BF16)
            source = grad_mem
        else:
            source = part_mem.at[0]
        stores = []
        if formed:
            stores.append(pltpu.make_async_copy(grad_mem, outs[0], store_sem.at[0]))
            stores[0].start()
        first = len(stores)
        blocks = [
            pltpu.make_async_copy(out_mem.at[b], outs[first + b], store_sem.at[first + b]) for b in range(len(order))
        ]

        @pl.loop(0, len(order))
        def _(b):
            pltpu.make_async_copy(weight_mem.at[b], weight_mem.at[b], load_sem.at[count + b]).wait()
            total = product(source[...].reshape(rows, width), weight_mem[b])

            @pl.when(order[0] - b != 0)
            def _():
                out_mem[b] = total.astype(BF16)

            @pl.when(order[0] - b == 0)
            def _():
                out_mem[b] = (total + source[...].reshape(rows, width).astype(F32)).astype(BF16)

            for n, block in enumerate(blocks):
                @pl.when(b == n)
                def _():
                    block.start()

        stores.extend(blocks)
        for store in stores:
            store.wait()


def products(active, where, parts, weights, order, formed, name, cost, after=()):
    shards, width, _ = weights.shape
    shape = parts[0].shape
    tokens = shape[0] * shape[1]
    loads = len(parts) + len(order)
    block = jax.ShapeDtypeStruct((tokens, width), BF16)
    return pl.pallas_call(
        functools.partial(products_kernel, active, order, len(parts), len(after), formed),
        in_specs=[pl.BlockSpec(memory_space=pltpu.SMEM)] + [ANY] * (len(parts) + 1 + len(after)),
        out_specs=[ANY] * (len(order) + formed),
        out_shape=[jax.ShapeDtypeStruct(shape, BF16)] * formed + [block] * len(order),
        scratch_shapes=[
            pltpu.VMEM((len(parts), *shape), BF16),
            pltpu.VMEM(shape, BF16),
            pltpu.VMEM((len(order), width, width), BF16),
            pltpu.VMEM((len(order), tokens, width), BF16),
            pltpu.SemaphoreType.DMA((loads,)),
            pltpu.SemaphoreType.DMA((len(order) + formed,)),
        ],
        compiler_params=params(),
        cost_estimate=cost,
        name=name,
    )(where, *parts, weights, *after)


def lead_products(active, where, parts, weights, after=()):
    return products(active, where, parts, weights, (3,), 1, "lead_products", BRIEF, after)


def rest_products(active, where, grad, weights, after=()):
    return products(active, where, (grad,), weights, (2, 1, 0), 0, "rest_products", LONG, after)


def add_kernel(active, where_ref, kept_ref, received_ref, *refs):
    out_ref, kept, received, total, sem = refs[-5:]

    @pl.when(where_ref[1] == active)
    def _():
        loads = [
            pltpu.make_async_copy(kept_ref, kept, sem.at[0]),
            pltpu.make_async_copy(received_ref, received, sem.at[1]),
        ]
        for load in loads:
            load.start()
        for load in loads:
            load.wait()
        total[...] = (kept[...].astype(F32) + received[...].astype(F32)).astype(BF16)
        store = pltpu.make_async_copy(total, out_ref, sem.at[2])
        store.start()
        store.wait()


def add_received(active, where, kept, received, after=()):
    return pl.pallas_call(
        functools.partial(add_kernel, active),
        in_specs=[pl.BlockSpec(memory_space=pltpu.SMEM)] + [ANY] * (2 + len(after)),
        out_specs=ANY,
        out_shape=jax.ShapeDtypeStruct(received.shape, BF16),
        scratch_shapes=[pltpu.VMEM(received.shape, BF16)] * 3 + [pltpu.SemaphoreType.DMA((3,))],
        compiler_params=params(ADD),
        cost_estimate=BRIEF,
        name="add_received",
    )(where, kept, received, *after)


def last_kernel(active, count, after, where_ref, *refs):
    parts, weight_ref, outs = refs[:count], refs[count], refs[count + 1 + after:-7]
    part_mem, grad_mem, weight_mem, out_mem, own_mem, load_sem, store_sem = refs[-7:]
    shards, rows, width = grad_mem.shape

    @pl.when(where_ref[1] == active)
    def _():
        part_loads = [
            pltpu.make_async_copy(part, part_mem.at[p], load_sem.at[p]) for p, part in enumerate(parts)
        ]
        weight_loads = [
            pltpu.make_async_copy(weight_ref.at[n], weight_mem.at[n], load_sem.at[count + n]) for n in range(shards)
        ]
        for load in part_loads + weight_loads:
            load.start()
        for load in part_loads:
            load.wait()
        total = part_mem[0].astype(F32)
        for p in range(1, count):
            total = total + part_mem[p].astype(F32)
        part_mem[0] = total.astype(BF16)
        stores = [pltpu.make_async_copy(part_mem.at[0], outs[0], store_sem.at[0])]
        stores[0].start()
        for k in range(shards):
            grad_mem[k] = part_mem[0, where_ref[0] ^ k]

        @pl.loop(0, shards)
        def _(n):
            pltpu.make_async_copy(weight_mem.at[n], weight_mem.at[n], load_sem.at[count + n]).wait()
            at = pl.ds(pl.multiple_of(n * width, 128), width)
            total = product(grad_mem[...].reshape(shards * rows, width), weight_mem[n])
            through = grad_mem[...].reshape(shards * rows, width).astype(F32)
            total = total + jnp.where(where_ref[0] == n, through, 0.0)
            own_mem[:, at] = total[:rows]
            for k in range(1, shards):
                out_mem[k - 1, :, at] = total[k * rows:(k + 1) * rows].astype(BF16)

        for k in range(1, shards):
            stores.append(pltpu.make_async_copy(out_mem.at[k - 1], outs[k], store_sem.at[k]))
        stores.append(pltpu.make_async_copy(own_mem, outs[shards], store_sem.at[shards]))
        for store in stores[1:]:
            store.start()
        for store in stores:
            store.wait()


def last_products(active, where, parts, weights, after=()):
    shards, width, _ = weights.shape
    shape = parts[0].shape
    rows = shape[1]
    half = jax.ShapeDtypeStruct((rows, shards * width), BF16)
    return pl.pallas_call(
        functools.partial(last_kernel, active, len(parts), len(after)),
        in_specs=[pl.BlockSpec(memory_space=pltpu.SMEM)] + [ANY] * (len(parts) + 1 + len(after)),
        out_specs=[ANY] * (shards + 1),
        out_shape=[jax.ShapeDtypeStruct(shape, BF16)]
        + [half] * (shards - 1)
        + [jax.ShapeDtypeStruct((rows, shards * width), F32)],
        scratch_shapes=[
            pltpu.VMEM((len(parts), *shape), BF16),
            pltpu.VMEM(shape, BF16),
            pltpu.VMEM(weights.shape, BF16),
            pltpu.VMEM((shards - 1, rows, shards * width), BF16),
            pltpu.VMEM((rows, shards * width), F32),
            pltpu.SemaphoreType.DMA((len(parts) + shards,)),
            pltpu.SemaphoreType.DMA((shards + 1,)),
        ],
        compiler_params=params(),
        cost_estimate=BRIEF,
        name="last_products",
    )(where, *parts, weights, *after)


def place_kernel(count, where_ref, *refs):
    pieces, outs = refs[:count], refs[count:]
    rows = outs[0].shape[1]
    for i, out_ref in enumerate(outs):
        for k, piece in enumerate(pieces):
            out_ref[where_ref[0] ^ k] = piece[i * rows:(i + 1) * rows]


def place_shards(where, pieces, chunks):
    tokens, width = pieces[0].shape
    memory = pl.BlockSpec(memory_space=pltpu.VMEM)
    return pl.pallas_call(
        functools.partial(place_kernel, len(pieces)),
        in_specs=[pl.BlockSpec(memory_space=pltpu.SMEM)] + [memory] * len(pieces),
        out_specs=[memory] * chunks,
        out_shape=[jax.ShapeDtypeStruct((len(pieces), tokens // chunks, width), BF16)] * chunks,
        compiler_params=params(SMALL),
        name="place_shards",
    )(where, *pieces)


def first_kernel(where_ref, *refs):
    out_ref = refs[-1]
    for i in range((len(refs) - 2) // 3):
        own, near, far = refs[3 * i:3 * i + 3]
        rows = own.shape[0]
        total = (own[...] + near[...].astype(F32) + far[...].astype(F32)).astype(BF16)
        out_ref[i * rows:(i + 1) * rows] = jnp.where(where_ref[1] == 0, total, jnp.zeros_like(total))


def first_inputs(where, sums, tokens, model, after):
    memory = pl.BlockSpec(memory_space=pltpu.VMEM)
    terms = [term for chunk in sums for term in chunk]
    return pl.pallas_call(
        first_kernel,
        in_specs=[pl.BlockSpec(memory_space=pltpu.SMEM)] + [memory] * len(terms) + [ANY],
        out_specs=memory,
        out_shape=jax.ShapeDtypeStruct((tokens, model), BF16),
        compiler_params=params(SMALL),
        cost_estimate=BRIEF,
        name="first_inputs",
    )(where, *terms, after)


def inputs_kernel(where_ref, sums_ref, *refs):
    pieces, out_ref = refs[:-1], refs[-1]
    width = pieces[0].shape[-1]
    for k, piece in enumerate(pieces):
        columns = pl.ds(pl.multiple_of((where_ref[0] ^ k) * width, 128), width)
        out_ref[:, columns] = sums_ref[:, columns] + piece[...]


def place_inputs(where, sums, pieces):
    memory = pl.BlockSpec(memory_space=pltpu.VMEM)
    return pl.pallas_call(
        inputs_kernel,
        in_specs=[pl.BlockSpec(memory_space=pltpu.SMEM)] + [memory] * (1 + len(pieces)),
        out_specs=memory,
        out_shape=jax.ShapeDtypeStruct(sums.shape, BF16),
        compiler_params=params(SMALL),
        name="place_inputs",
    )(where, sums, *pieces)


def cut_kernel(owners, chunks, where_ref, *refs):
    held, sem = refs[-2:]
    shards = held.shape[0]
    outs = refs[-2 - shards:-2]
    rows = refs[0].shape[1]
    for o, section in enumerate(owners):
        grads = refs[o * chunks:(o + 1) * chunks]

        @pl.when(where_ref[1] == section)
        def _():
            loads = [
                pltpu.make_async_copy(grad.at[where_ref[0] ^ k], held.at[k, pl.ds(i * rows, rows)], sem.at[k, i])
                for k in range(shards)
                for i, grad in enumerate(grads)
            ]
            for load in loads:
                load.start()
            for load in loads:
                load.wait()
            stores = [pltpu.make_async_copy(held.at[k], out, sem.at[k, 0]) for k, out in enumerate(outs)]
            for store in stores:
                store.start()
            for store in stores:
                store.wait()


def cut_shards(where, owners, after):
    grads = [grad for _, chunk in owners for grad in chunk]
    chunks = len(owners[0][1])
    shards, rows, width = grads[0].shape
    tokens = rows * chunks
    return pl.pallas_call(
        functools.partial(cut_kernel, [section for section, _ in owners], chunks),
        in_specs=[pl.BlockSpec(memory_space=pltpu.SMEM)] + [ANY] * (len(grads) + len(after)),
        out_specs=[ANY] * shards,
        out_shape=[jax.ShapeDtypeStruct((tokens, width), BF16)] * shards,
        scratch_shapes=[
            pltpu.VMEM((shards, tokens, width), BF16),
            pltpu.SemaphoreType.DMA((shards, chunks)),
        ],
        compiler_params=params(SMALL),
        cost_estimate=BRIEF,
        name="cut_shards",
    )(where, *grads, *after)


def pick_kernel(owners, chunks, where_ref, *refs):
    out_ref, held, sem = refs[-3:]
    for o, section in enumerate(owners):
        grads = refs[o * chunks:(o + 1) * chunks]

        @pl.when(where_ref[1] == section)
        def _():
            loads = [pltpu.make_async_copy(grad, held.at[i], sem.at[i]) for i, grad in enumerate(grads)]
            for load in loads:
                load.start()
            for load in loads:
                load.wait()
            store = pltpu.make_async_copy(held, out_ref, sem.at[0])
            store.start()
            store.wait()


def pick(where, owners, after):
    grads = [grad for _, chunk in owners for grad in chunk]
    shape = (len(owners[0][1]), *grads[0].shape)
    return pl.pallas_call(
        functools.partial(pick_kernel, [section for section, _ in owners], shape[0]),
        in_specs=[pl.BlockSpec(memory_space=pltpu.SMEM)] + [ANY] * (len(grads) + len(after)),
        out_specs=ANY,
        out_shape=jax.ShapeDtypeStruct(shape, BF16),
        scratch_shapes=[pltpu.VMEM(shape, BF16), pltpu.SemaphoreType.DMA(shape[:1])],
        compiler_params=params(SMALL),
        cost_estimate=BRIEF,
        name="pick",
    )(where, *grads, *after)


def mark_kernel(*refs):
    refs[-1][...] = jnp.zeros_like(refs[-1])


def mark(cost, *after):
    return pl.pallas_call(
        mark_kernel,
        in_specs=[ANY] * len(after),
        out_specs=pl.BlockSpec(memory_space=pltpu.VMEM),
        out_shape=jax.ShapeDtypeStruct((8, 128), F32),
        compiler_params=params(SMALL),
        cost_estimate=cost,
        name="mark",
    )(*after)


def join_kernel(sections, count, where_ref, *refs):
    parts, out_ref, held, sem = refs[:count], refs[-3], refs[-2], refs[-1]
    rows = parts[0].shape[0]

    @pl.when((where_ref[1] >= sections[0]) & (where_ref[1] <= sections[-1]))
    def _():
        loads = [
            pltpu.make_async_copy(part, held.at[pl.ds(j * rows, rows)], sem.at[j]) for j, part in enumerate(parts)
        ]
        for load in loads:
            load.start()
        for load in loads:
            load.wait()
        store = pltpu.make_async_copy(held, out_ref, sem.at[0])
        store.start()
        store.wait()


def join(sections, where, parts, after):
    rows, width = parts[0].shape
    return pl.pallas_call(
        functools.partial(join_kernel, sections, len(parts)),
        in_specs=[pl.BlockSpec(memory_space=pltpu.SMEM)] + [ANY] * (len(parts) + 1),
        out_specs=ANY,
        out_shape=jax.ShapeDtypeStruct((rows * len(parts), width), BF16),
        scratch_shapes=[pltpu.VMEM((rows * len(parts), width), BF16), pltpu.SemaphoreType.DMA((len(parts),))],
        compiler_params=params(SMALL),
        cost_estimate=BRIEF,
        name="join",
    )(where, *parts, after)


def weight_kernel(owners, half, sections, shards, replicas, chunks, where_ref, *refs):
    groups, grads = refs[:len(owners) * shards], refs[len(owners) * shards:-6]
    out_ref, saved, ordered, out_mem, load_sem, store_sem = refs[-6:]
    _, rows, width = grads[0].shape
    tokens = chunks * rows
    step = out_mem.shape[1]
    steps = out_ref.shape[0] // step

    loads = []
    for k in range(shards):
        for g, owner in enumerate(owners):
            @pl.when((where_ref[1] >= owner[0]) & (where_ref[1] <= owner[-1]))
            def _():
                pltpu.make_async_copy(groups[g * shards + k], saved.at[k], load_sem.at[k]).start()

        loads.append(pltpu.make_async_copy(groups[k], saved.at[k], load_sem.at[k]))
    def grad_loads(section):
        for k in range(shards):
            for j in range(replicas):
                for i in range(chunks):
                    if j == 0:
                        grad = grads[section * chunks + i]
                    elif section == 0:
                        grad = grads[(sections + j - 1) * chunks + i]
                    else:
                        later = (replicas - 1) * (section >= half)
                        grad = grads[(sections + replicas - 1) * chunks + later + j - 1].at[i]
                    at = (k * replicas + j) * tokens + i * rows
                    yield pltpu.make_async_copy(
                        grad.at[where_ref[0] ^ k],
                        ordered.at[pl.ds(at, rows)],
                        load_sem.at[shards + (k * replicas + j) * chunks + i],
                    )

    for section in range(sections):
        @pl.when(where_ref[1] == section)
        def _():
            for load in grad_loads(section):
                load.start()

    loads.extend(grad_loads(0))
    for load in loads:
        load.wait()

    def store(n):
        slot = lax.rem(n, 2)
        return pltpu.make_async_copy(
            out_mem.at[slot], out_ref.at[pl.ds(pl.multiple_of(n * step, step), step)], store_sem.at[slot]
        )

    @pl.loop(0, steps)
    def _(n):
        @pl.when(n >= 2)
        def _():
            store(n - 2).wait()

        features = pl.ds(pl.multiple_of(n * step, step), step)
        out_mem[lax.rem(n, 2)] = lax.dot_general(
            saved[:, :, features].reshape(ordered.shape[0], step),
            ordered[...],
            (((0,), (0,)), ((), ())),
            preferred_element_type=F32,
        )
        store(n).start()

    for n in range(max(steps - 2, 0), steps):
        store(n).wait()


def weight_products(where, gathered, half, own_grads, first_peers, other_peers):
    owners = tuple(tuple(sections) for sections, _ in gathered)
    groups = [array for _, arrays in gathered for array in arrays]
    shards = len(gathered[0][1])
    tokens, features = groups[0].shape
    sections, replicas = len(own_grads), len(first_peers) + 1
    chunks, width = len(own_grads[0]), own_grads[0][0].shape[-1]
    grads = [grad for chunk in (*own_grads, *first_peers) for grad in chunk] + other_peers
    step = divisor(features, (256, 128))
    return pl.pallas_call(
        functools.partial(weight_kernel, owners, half, sections, shards, replicas, chunks),
        in_specs=[pl.BlockSpec(memory_space=pltpu.SMEM)] + [ANY] * (len(groups) + len(grads)),
        out_specs=ANY,
        out_shape=jax.ShapeDtypeStruct((features, width), F32),
        scratch_shapes=[
            pltpu.VMEM((shards, tokens, features), BF16),
            pltpu.VMEM((shards * tokens, width), BF16),
            pltpu.VMEM((2, step, width), F32),
            pltpu.SemaphoreType.DMA((shards + shards * replicas * chunks,)),
            pltpu.SemaphoreType.DMA((2,)),
        ],
        compiler_params=params(),
        cost_estimate=BRIEF,
        name="weight_products",
    )(where, *groups, *grads)


def on_device(sections, replicas, shards, saved, weight, out_grad):
    tokens, model = out_grad.shape
    width = model // shards
    chunks = CHUNKS
    rows = tokens // chunks
    section, dp, tensor = (lax.axis_index(a) for a in AXES)
    weights = weight[0].reshape(shards, width, width)
    activations = saved[0]

    def place(s, d, t):
        return (s * replicas + d) * shards + t

    def permute(value, route, active):
        pairs = []
        for s in active:
            for d in range(replicas):
                for t in range(shards):
                    to = route(s, d, t)
                    if 0 <= to[0] < sections:
                        pairs.append((place(s, d, t), place(*to)))
        return lax.ppermute(value, AXES, pairs)

    def across(k):
        return lambda s, d, t: (s, d, t ^ k)

    everyone = range(sections)
    where = jnp.stack([tensor, section]).astype(jnp.int32)

    last = sections - 1
    pieces = [lax.dynamic_slice(out_grad, (0, tensor * width), (tokens, width))]
    for k in range(1, shards):
        block = lax.dynamic_slice(out_grad, (0, (tensor ^ k) * width), (tokens, width))
        pieces.append(permute(block, across(k), [last]))
    first = place_shards(where, pieces, chunks)

    height = model // replicas
    own_rows = [lax.dynamic_slice(activations, (0, dp * height), (tokens, height))]
    for j in range(1, replicas):
        block = lax.dynamic_slice(activations, (0, lax.rem(dp + replicas - j, replicas) * height), (tokens, height))
        own_rows.append(
            permute(block, lambda s, d, t: (s, (d - j) % replicas, t), everyone)
        )

    def swap(value, active):
        return [permute(value, lambda s, d, t: (s, (d - j) % replicas, t), active) for j in range(1, replicas)]

    half = sections // 2
    low, high = range(half), range(half, sections)
    def gather(value, active):
        near, far = permute(value, across(1), active), permute(value, across(2), active)
        return [value, near, far, permute(far, across(1), active)]

    gathered, kept = [(low, gather(join(low, where, own_rows, first[0]), low))], []
    swapped = []
    due = {(0, 1): gathered[0][1][1:3], (half, 0): gathered[0][1][3:]}
    incoming = [(first[i],) for i in range(chunks)]
    ended = ()
    for r in range(sections - 1):
        active = sections - 1 - r
        grads, outgoing = [], []
        for i in range(chunks):
            before = outgoing[-1] if i else incoming[-1] if r else ()
            pinned = (*before[:2], *due.get((r, i), ()))
            grad, lead = lead_products(active, where, incoming[i], weights, ended)
            received = permute(lead, across(1), [active])
            if active == half - 1 and i == chunks - 1:
                token = permute(mark(BRIEF, grad), lambda s, d, t: (s + 1, d, t), range(half - 1, sections - 1))
                gathered.append((high, gather(join(high, where, own_rows, token), high)))
                pinned = (*pinned, token)
            keep, near, own = rest_products(active, where, grad, weights, pinned)
            sums = [
                permute(own.reshape(grad.shape), lambda s, d, t: (s - 1, d, t), [active]),
                permute(near.reshape(grad.shape), lambda s, d, t: (s - 1, d, t ^ 1), [active]),
            ]
            stop = (mark(LONG, keep, before[2]),) if i else (near,)
            part = add_received(active, where, keep, received, stop)
            sums.append(permute(part.reshape(grad.shape), lambda s, d, t: (s - 1, d, t ^ 2), [active]))
            ended = (part,)
            outgoing.append(sums)
            grads.append(grad)
        incoming = outgoing
        kept.append(grads)

    def send_back(owners, after):
        blocks = cut_shards(where, [(s, kept[sections - 1 - s]) for s in owners], after)
        return [permute(block, lambda s, d, t: (s + 1, d, t ^ k), owners) for k, block in enumerate(blocks)]

    first_products, finals, last_grads = [], [], []
    picked = pick(where, [(s, kept[sections - 1 - s]) for s in high], ended)
    others = swap(picked, high)
    ended = (*ended, *gathered[-1][1][1:3], *others)
    for i in range(chunks):
        grad, near, keep, lead, own = last_products(0, where, incoming[i], weights, ended)
        first_products.append((keep, permute(lead, across(1), [0])))
        finals.append([own, permute(near, across(1), [0])])
        swapped.append(swap(grad, [0]))
        if not i:
            picked = pick(where, [(s, kept[sections - 1 - s]) for s in low[1:]], (grad,))
            others = swap(picked, low[1:]) + others
            ended = (mark(LONG, keep, *incoming[-1], finals[0][1]),)
        last_grads.append(grad)
    kept.append(last_grads)
    ended = (keep,)
    for i, (keep, received) in enumerate(first_products):
        if i:
            ended = (mark(LONG, *ended, received, *swapped[0], *others[:replicas - 1]),)
        part = add_received(0, where, keep, received, ended)
        finals[i].append(permute(part, across(2), [0]))
        ended = (part,)

    back = send_back(range(sections - 1), (part, finals[-1][1], *swapped[-1]))
    weight_grad = weight_products(where, gathered, half, kept[::-1], list(zip(*swapped)), others)
    own_input = place_inputs(where, first_inputs(where, finals, tokens, model, weight_grad), back)
    return (own_input[None], weight_grad[None])


def solution(mesh):
    placed = (
        P("section", ("dp", "tensor"), None),
        P("section", None, "tensor"),
        P(("dp", "tensor"), None),
    )
    sizes = [mesh.shape[a] for a in AXES]
    return jax.shard_map(
        functools.partial(on_device, *sizes),
        mesh=mesh,
        in_specs=placed,
        out_specs=(P("section", ("dp", "tensor"), None), P("section", "dp", "tensor")),
        check_vma=False,
    )
```

```python
import functools

import jax
import jax.numpy as jnp
from jax import lax
from jax.experimental import pallas as pl
from jax.experimental.pallas import tpu as pltpu
from jax.sharding import PartitionSpec as P

AXES = ("section", "dp", "tensor")
CHUNKS = 2
VMEM = 56 * 1024 * 1024
ADD = 56 * 1024 * 1024
SMALL = 56 * 1024 * 1024
F32 = jnp.float32
BF16 = jnp.bfloat16
LONG = pl.CostEstimate(flops=200000000000, bytes_accessed=1000, transcendentals=0)
BRIEF = pl.CostEstimate(flops=1000, bytes_accessed=1000, transcendentals=0)
ANY = pl.BlockSpec(memory_space=pl.ANY)


def params(limit=VMEM):
    return pltpu.CompilerParams(vmem_limit_bytes=limit)


def divisor(total, options):
    for option in options:
        if total % option == 0:
            return option
    return total


def product(lhs, rhs):
    return lax.dot_general(lhs, rhs, (((1,), (1,)), ((), ())), preferred_element_type=F32)


def products_kernel(active, order, count, after, formed, where_ref, *refs):
    parts, weight_ref, outs = refs[:count], refs[count], refs[count + 1 + after:-6]
    part_mem, grad_mem, weight_mem, out_mem, load_sem, store_sem = refs[-6:]
    rows, width = grad_mem.shape[0] * grad_mem.shape[1], grad_mem.shape[2]

    @pl.when(where_ref[1] == active)
    def _():
        part_loads = [
            pltpu.make_async_copy(part, part_mem.at[p], load_sem.at[p]) for p, part in enumerate(parts)
        ]
        weight_loads = [
            pltpu.make_async_copy(weight_ref.at[where_ref[0] ^ k], weight_mem.at[b], load_sem.at[count + b])
            for b, k in enumerate(order)
        ]
        for load in part_loads + weight_loads:
            load.start()
        for load in part_loads:
            load.wait()
        if formed:
            total = part_mem[0].astype(F32)
            for p in range(1, count):
                total = total + part_mem[p].astype(F32)
            grad_mem[...] = total.astype(BF16)
            source = grad_mem
        else:
            source = part_mem.at[0]
        stores = []
        if formed:
            stores.append(pltpu.make_async_copy(grad_mem, outs[0], store_sem.at[0]))
            stores[0].start()
        first = len(stores)
        blocks = [
            pltpu.make_async_copy(out_mem.at[b], outs[first + b], store_sem.at[first + b]) for b in range(len(order))
        ]

        @pl.loop(0, len(order))
        def _(b):
            pltpu.make_async_copy(weight_mem.at[b], weight_mem.at[b], load_sem.at[count + b]).wait()
            total = product(source[...].reshape(rows, width), weight_mem[b])

            @pl.when(order[0] - b != 0)
            def _():
                out_mem[b] = total.astype(BF16)

            @pl.when(order[0] - b == 0)
            def _():
                out_mem[b] = (total + source[...].reshape(rows, width).astype(F32)).astype(BF16)

            for n, block in enumerate(blocks):
                @pl.when(b == n)
                def _():
                    block.start()

        stores.extend(blocks)
        for store in stores:
            store.wait()


def products(active, where, parts, weights, order, formed, name, cost, after=()):
    shards, width, _ = weights.shape
    shape = parts[0].shape
    tokens = shape[0] * shape[1]
    loads = len(parts) + len(order)
    block = jax.ShapeDtypeStruct((tokens, width), BF16)
    return pl.pallas_call(
        functools.partial(products_kernel, active, order, len(parts), len(after), formed),
        in_specs=[pl.BlockSpec(memory_space=pltpu.SMEM)] + [ANY] * (len(parts) + 1 + len(after)),
        out_specs=[ANY] * (len(order) + formed),
        out_shape=[jax.ShapeDtypeStruct(shape, BF16)] * formed + [block] * len(order),
        scratch_shapes=[
            pltpu.VMEM((len(parts), *shape), BF16),
            pltpu.VMEM(shape, BF16),
            pltpu.VMEM((len(order), width, width), BF16),
            pltpu.VMEM((len(order), tokens, width), BF16),
            pltpu.SemaphoreType.DMA((loads,)),
            pltpu.SemaphoreType.DMA((len(order) + formed,)),
        ],
        compiler_params=params(),
        cost_estimate=cost,
        name=name,
    )(where, *parts, weights, *after)


def lead_products(active, where, parts, weights, after=()):
    return products(active, where, parts, weights, (3,), 1, "lead_products", BRIEF, after)


def rest_products(active, where, grad, weights, after=()):
    return products(active, where, (grad,), weights, (2, 1, 0), 0, "rest_products", LONG, after)


def add_kernel(active, where_ref, kept_ref, received_ref, *refs):
    out_ref, kept, received, total, sem = refs[-5:]

    @pl.when(where_ref[1] == active)
    def _():
        loads = [
            pltpu.make_async_copy(kept_ref, kept, sem.at[0]),
            pltpu.make_async_copy(received_ref, received, sem.at[1]),
        ]
        for load in loads:
            load.start()
        for load in loads:
            load.wait()
        total[...] = (kept[...].astype(F32) + received[...].astype(F32)).astype(BF16)
        store = pltpu.make_async_copy(total, out_ref, sem.at[2])
        store.start()
        store.wait()


def add_received(active, where, kept, received, after=()):
    return pl.pallas_call(
        functools.partial(add_kernel, active),
        in_specs=[pl.BlockSpec(memory_space=pltpu.SMEM)] + [ANY] * (2 + len(after)),
        out_specs=ANY,
        out_shape=jax.ShapeDtypeStruct(received.shape, BF16),
        scratch_shapes=[pltpu.VMEM(received.shape, BF16)] * 3 + [pltpu.SemaphoreType.DMA((3,))],
        compiler_params=params(ADD),
        cost_estimate=BRIEF,
        name="add_received",
    )(where, kept, received, *after)


def last_kernel(active, count, after, where_ref, *refs):
    parts, weight_ref, outs = refs[:count], refs[count], refs[count + 1 + after:-7]
    part_mem, grad_mem, weight_mem, out_mem, own_mem, load_sem, store_sem = refs[-7:]
    shards, rows, width = grad_mem.shape

    @pl.when(where_ref[1] == active)
    def _():
        part_loads = [
            pltpu.make_async_copy(part, part_mem.at[p], load_sem.at[p]) for p, part in enumerate(parts)
        ]
        weight_loads = [
            pltpu.make_async_copy(weight_ref.at[n], weight_mem.at[n], load_sem.at[count + n]) for n in range(shards)
        ]
        for load in part_loads + weight_loads:
            load.start()
        for load in part_loads:
            load.wait()
        total = part_mem[0].astype(F32)
        for p in range(1, count):
            total = total + part_mem[p].astype(F32)
        part_mem[0] = total.astype(BF16)
        stores = [pltpu.make_async_copy(part_mem.at[0], outs[0], store_sem.at[0])]
        stores[0].start()
        for k in range(shards):
            grad_mem[k] = part_mem[0, where_ref[0] ^ k]

        @pl.loop(0, shards)
        def _(n):
            pltpu.make_async_copy(weight_mem.at[n], weight_mem.at[n], load_sem.at[count + n]).wait()
            at = pl.ds(pl.multiple_of(n * width, 128), width)
            total = product(grad_mem[...].reshape(shards * rows, width), weight_mem[n])
            through = grad_mem[...].reshape(shards * rows, width).astype(F32)
            total = total + jnp.where(where_ref[0] == n, through, 0.0)
            own_mem[:, at] = total[:rows]
            for k in range(1, shards):
                out_mem[k - 1, :, at] = total[k * rows:(k + 1) * rows].astype(BF16)

        for k in range(1, shards):
            stores.append(pltpu.make_async_copy(out_mem.at[k - 1], outs[k], store_sem.at[k]))
        stores.append(pltpu.make_async_copy(own_mem, outs[shards], store_sem.at[shards]))
        for store in stores[1:]:
            store.start()
        for store in stores:
            store.wait()


def last_products(active, where, parts, weights, after=()):
    shards, width, _ = weights.shape
    shape = parts[0].shape
    rows = shape[1]
    half = jax.ShapeDtypeStruct((rows, shards * width), BF16)
    return pl.pallas_call(
        functools.partial(last_kernel, active, len(parts), len(after)),
        in_specs=[pl.BlockSpec(memory_space=pltpu.SMEM)] + [ANY] * (len(parts) + 1 + len(after)),
        out_specs=[ANY] * (shards + 1),
        out_shape=[jax.ShapeDtypeStruct(shape, BF16)]
        + [half] * (shards - 1)
        + [jax.ShapeDtypeStruct((rows, shards * width), F32)],
        scratch_shapes=[
            pltpu.VMEM((len(parts), *shape), BF16),
            pltpu.VMEM(shape, BF16),
            pltpu.VMEM(weights.shape, BF16),
            pltpu.VMEM((shards - 1, rows, shards * width), BF16),
            pltpu.VMEM((rows, shards * width), F32),
            pltpu.SemaphoreType.DMA((len(parts) + shards,)),
            pltpu.SemaphoreType.DMA((shards + 1,)),
        ],
        compiler_params=params(),
        cost_estimate=BRIEF,
        name="last_products",
    )(where, *parts, weights, *after)


def place_kernel(count, where_ref, *refs):
    pieces, outs = refs[:count], refs[count:]
    rows = outs[0].shape[1]
    for i, out_ref in enumerate(outs):
        for k, piece in enumerate(pieces):
            out_ref[where_ref[0] ^ k] = piece[i * rows:(i + 1) * rows]


def place_shards(where, pieces, chunks):
    tokens, width = pieces[0].shape
    memory = pl.BlockSpec(memory_space=pltpu.VMEM)
    return pl.pallas_call(
        functools.partial(place_kernel, len(pieces)),
        in_specs=[pl.BlockSpec(memory_space=pltpu.SMEM)] + [memory] * len(pieces),
        out_specs=[memory] * chunks,
        out_shape=[jax.ShapeDtypeStruct((len(pieces), tokens // chunks, width), BF16)] * chunks,
        compiler_params=params(SMALL),
        name="place_shards",
    )(where, *pieces)


def first_kernel(where_ref, *refs):
    out_ref = refs[-1]
    for i in range((len(refs) - 2) // 3):
        own, near, far = refs[3 * i:3 * i + 3]
        rows = own.shape[0]
        total = (own[...] + near[...].astype(F32) + far[...].astype(F32)).astype(BF16)
        out_ref[i * rows:(i + 1) * rows] = jnp.where(where_ref[1] == 0, total, jnp.zeros_like(total))


def first_inputs(where, sums, tokens, model, after):
    memory = pl.BlockSpec(memory_space=pltpu.VMEM)
    terms = [term for chunk in sums for term in chunk]
    return pl.pallas_call(
        first_kernel,
        in_specs=[pl.BlockSpec(memory_space=pltpu.SMEM)] + [memory] * len(terms) + [ANY],
        out_specs=memory,
        out_shape=jax.ShapeDtypeStruct((tokens, model), BF16),
        compiler_params=params(SMALL),
        cost_estimate=BRIEF,
        name="first_inputs",
    )(where, *terms, after)


def inputs_kernel(where_ref, sums_ref, *refs):
    pieces, out_ref = refs[:-1], refs[-1]
    width = pieces[0].shape[-1]
    for k, piece in enumerate(pieces):
        columns = pl.ds(pl.multiple_of((where_ref[0] ^ k) * width, 128), width)
        out_ref[:, columns] = sums_ref[:, columns] + piece[...]


def place_inputs(where, sums, pieces):
    memory = pl.BlockSpec(memory_space=pltpu.VMEM)
    return pl.pallas_call(
        inputs_kernel,
        in_specs=[pl.BlockSpec(memory_space=pltpu.SMEM)] + [memory] * (1 + len(pieces)),
        out_specs=memory,
        out_shape=jax.ShapeDtypeStruct(sums.shape, BF16),
        compiler_params=params(SMALL),
        name="place_inputs",
    )(where, sums, *pieces)


def cut_kernel(owners, chunks, where_ref, *refs):
    held, sem = refs[-2:]
    shards = held.shape[0]
    outs = refs[-2 - shards:-2]
    rows = refs[0].shape[1]
    for o, section in enumerate(owners):
        grads = refs[o * chunks:(o + 1) * chunks]

        @pl.when(where_ref[1] == section)
        def _():
            loads = [
                pltpu.make_async_copy(grad.at[where_ref[0] ^ k], held.at[k, pl.ds(i * rows, rows)], sem.at[k, i])
                for k in range(shards)
                for i, grad in enumerate(grads)
            ]
            for load in loads:
                load.start()
            for load in loads:
                load.wait()
            stores = [pltpu.make_async_copy(held.at[k], out, sem.at[k, 0]) for k, out in enumerate(outs)]
            for store in stores:
                store.start()
            for store in stores:
                store.wait()


def cut_shards(where, owners, after):
    grads = [grad for _, chunk in owners for grad in chunk]
    chunks = len(owners[0][1])
    shards, rows, width = grads[0].shape
    tokens = rows * chunks
    return pl.pallas_call(
        functools.partial(cut_kernel, [section for section, _ in owners], chunks),
        in_specs=[pl.BlockSpec(memory_space=pltpu.SMEM)] + [ANY] * (len(grads) + len(after)),
        out_specs=[ANY] * shards,
        out_shape=[jax.ShapeDtypeStruct((tokens, width), BF16)] * shards,
        scratch_shapes=[
            pltpu.VMEM((shards, tokens, width), BF16),
            pltpu.SemaphoreType.DMA((shards, chunks)),
        ],
        compiler_params=params(SMALL),
        cost_estimate=BRIEF,
        name="cut_shards",
    )(where, *grads, *after)


def pick_kernel(owners, chunks, where_ref, *refs):
    out_ref, held, sem = refs[-3:]
    for o, section in enumerate(owners):
        grads = refs[o * chunks:(o + 1) * chunks]

        @pl.when(where_ref[1] == section)
        def _():
            loads = [pltpu.make_async_copy(grad, held.at[i], sem.at[i]) for i, grad in enumerate(grads)]
            for load in loads:
                load.start()
            for load in loads:
                load.wait()
            store = pltpu.make_async_copy(held, out_ref, sem.at[0])
            store.start()
            store.wait()


def pick(where, owners, after):
    grads = [grad for _, chunk in owners for grad in chunk]
    shape = (len(owners[0][1]), *grads[0].shape)
    return pl.pallas_call(
        functools.partial(pick_kernel, [section for section, _ in owners], shape[0]),
        in_specs=[pl.BlockSpec(memory_space=pltpu.SMEM)] + [ANY] * (len(grads) + len(after)),
        out_specs=ANY,
        out_shape=jax.ShapeDtypeStruct(shape, BF16),
        scratch_shapes=[pltpu.VMEM(shape, BF16), pltpu.SemaphoreType.DMA(shape[:1])],
        compiler_params=params(SMALL),
        cost_estimate=BRIEF,
        name="pick",
    )(where, *grads, *after)


def mark_kernel(*refs):
    refs[-1][...] = jnp.zeros_like(refs[-1])


def mark(cost, *after):
    return pl.pallas_call(
        mark_kernel,
        in_specs=[ANY] * len(after),
        out_specs=pl.BlockSpec(memory_space=pltpu.VMEM),
        out_shape=jax.ShapeDtypeStruct((8, 128), F32),
        compiler_params=params(SMALL),
        cost_estimate=cost,
        name="mark",
    )(*after)


def join_kernel(sections, count, where_ref, *refs):
    parts, out_ref, held, sem = refs[:count], refs[-3], refs[-2], refs[-1]
    rows = parts[0].shape[0]

    @pl.when((where_ref[1] >= sections[0]) & (where_ref[1] <= sections[-1]))
    def _():
        loads = [
            pltpu.make_async_copy(part, held.at[pl.ds(j * rows, rows)], sem.at[j]) for j, part in enumerate(parts)
        ]
        for load in loads:
            load.start()
        for load in loads:
            load.wait()
        store = pltpu.make_async_copy(held, out_ref, sem.at[0])
        store.start()
        store.wait()


def join(sections, where, parts, after):
    rows, width = parts[0].shape
    return pl.pallas_call(
        functools.partial(join_kernel, sections, len(parts)),
        in_specs=[pl.BlockSpec(memory_space=pltpu.SMEM)] + [ANY] * (len(parts) + 1),
        out_specs=ANY,
        out_shape=jax.ShapeDtypeStruct((rows * len(parts), width), BF16),
        scratch_shapes=[pltpu.VMEM((rows * len(parts), width), BF16), pltpu.SemaphoreType.DMA((len(parts),))],
        compiler_params=params(SMALL),
        cost_estimate=BRIEF,
        name="join",
    )(where, *parts, after)


def weight_kernel(owners, half, sections, shards, replicas, chunks, where_ref, *refs):
    groups, grads = refs[:len(owners) * shards], refs[len(owners) * shards:-6]
    out_ref, saved, ordered, out_mem, load_sem, store_sem = refs[-6:]
    _, rows, width = grads[0].shape
    tokens = chunks * rows
    step = out_mem.shape[1]
    steps = out_ref.shape[0] // step

    loads = []
    for k in range(shards):
        for g, owner in enumerate(owners):
            @pl.when((where_ref[1] >= owner[0]) & (where_ref[1] <= owner[-1]))
            def _():
                pltpu.make_async_copy(groups[g * shards + k], saved.at[k], load_sem.at[k]).start()

        loads.append(pltpu.make_async_copy(groups[k], saved.at[k], load_sem.at[k]))
    def grad_loads(section):
        for k in range(shards):
            for j in range(replicas):
                for i in range(chunks):
                    if j == 0:
                        grad = grads[section * chunks + i]
                    elif section == 0:
                        grad = grads[(sections + j - 1) * chunks + i]
                    else:
                        later = (replicas - 1) * (section >= half)
                        grad = grads[(sections + replicas - 1) * chunks + later + j - 1].at[i]
                    at = (k * replicas + j) * tokens + i * rows
                    yield pltpu.make_async_copy(
                        grad.at[where_ref[0] ^ k],
                        ordered.at[pl.ds(at, rows)],
                        load_sem.at[shards + (k * replicas + j) * chunks + i],
                    )

    for section in range(sections):
        @pl.when(where_ref[1] == section)
        def _():
            for load in grad_loads(section):
                load.start()

    loads.extend(grad_loads(0))
    for load in loads:
        load.wait()

    def store(n):
        slot = lax.rem(n, 2)
        return pltpu.make_async_copy(
            out_mem.at[slot], out_ref.at[pl.ds(pl.multiple_of(n * step, step), step)], store_sem.at[slot]
        )

    @pl.loop(0, steps)
    def _(n):
        @pl.when(n >= 2)
        def _():
            store(n - 2).wait()

        features = pl.ds(pl.multiple_of(n * step, step), step)
        out_mem[lax.rem(n, 2)] = lax.dot_general(
            saved[:, :, features].reshape(ordered.shape[0], step),
            ordered[...],
            (((0,), (0,)), ((), ())),
            preferred_element_type=F32,
        )
        store(n).start()

    for n in range(max(steps - 2, 0), steps):
        store(n).wait()


def weight_products(where, gathered, half, own_grads, first_peers, other_peers):
    owners = tuple(tuple(sections) for sections, _ in gathered)
    groups = [array for _, arrays in gathered for array in arrays]
    shards = len(gathered[0][1])
    tokens, features = groups[0].shape
    sections, replicas = len(own_grads), len(first_peers) + 1
    chunks, width = len(own_grads[0]), own_grads[0][0].shape[-1]
    grads = [grad for chunk in (*own_grads, *first_peers) for grad in chunk] + other_peers
    step = divisor(features, (256, 128))
    return pl.pallas_call(
        functools.partial(weight_kernel, owners, half, sections, shards, replicas, chunks),
        in_specs=[pl.BlockSpec(memory_space=pltpu.SMEM)] + [ANY] * (len(groups) + len(grads)),
        out_specs=ANY,
        out_shape=jax.ShapeDtypeStruct((features, width), F32),
        scratch_shapes=[
            pltpu.VMEM((shards, tokens, features), BF16),
            pltpu.VMEM((shards * tokens, width), BF16),
            pltpu.VMEM((2, step, width), F32),
            pltpu.SemaphoreType.DMA((shards + shards * replicas * chunks,)),
            pltpu.SemaphoreType.DMA((2,)),
        ],
        compiler_params=params(),
        cost_estimate=BRIEF,
        name="weight_products",
    )(where, *groups, *grads)


def on_device(sections, replicas, shards, saved, weight, out_grad):
    tokens, model = out_grad.shape
    width = model // shards
    chunks = CHUNKS
    rows = tokens // chunks
    section, dp, tensor = (lax.axis_index(a) for a in AXES)
    weights = weight[0].reshape(shards, width, width)
    activations = saved[0]

    def place(s, d, t):
        return (s * replicas + d) * shards + t

    def permute(value, route, active):
        pairs = []
        for s in active:
            for d in range(replicas):
                for t in range(shards):
                    to = route(s, d, t)
                    if 0 <= to[0] < sections:
                        pairs.append((place(s, d, t), place(*to)))
        return lax.ppermute(value, AXES, pairs)

    def across(k):
        return lambda s, d, t: (s, d, t ^ k)

    everyone = range(sections)
    where = jnp.stack([tensor, section]).astype(jnp.int32)

    last = sections - 1
    pieces = [lax.dynamic_slice(out_grad, (0, tensor * width), (tokens, width))]
    for k in range(1, shards):
        block = lax.dynamic_slice(out_grad, (0, (tensor ^ k) * width), (tokens, width))
        pieces.append(permute(block, across(k), [last]))
    first = place_shards(where, pieces, chunks)

    height = model // replicas
    own_rows = [lax.dynamic_slice(activations, (0, dp * height), (tokens, height))]
    for j in range(1, replicas):
        block = lax.dynamic_slice(activations, (0, lax.rem(dp + replicas - j, replicas) * height), (tokens, height))
        own_rows.append(
            permute(block, lambda s, d, t: (s, (d - j) % replicas, t), everyone)
        )

    def swap(value, active):
        return [permute(value, lambda s, d, t: (s, (d - j) % replicas, t), active) for j in range(1, replicas)]

    half = sections // 2
    low, high = range(half), range(half, sections)
    def gather(value, active):
        near, far = permute(value, across(1), active), permute(value, across(2), active)
        return [value, near, far, permute(far, across(1), active)]

    gathered, kept = [(low, gather(join(low, where, own_rows, first[0]), low))], []
    swapped = []
    due = {(0, 1): gathered[0][1][1:3], (half, 0): gathered[0][1][3:]}
    incoming = [(first[i],) for i in range(chunks)]
    ended = ()
    for r in range(sections - 1):
        active = sections - 1 - r
        grads, outgoing = [], []
        for i in range(chunks):
            before = outgoing[-1] if i else incoming[-1] if r else ()
            turn = i and active == half - 1
            pinned = (*(before if turn else before[:2]), *due.get((r, i), ()))
            grad, lead = lead_products(active, where, incoming[i], weights, ended)
            received = permute(lead, across(1), [active])
            if active == half - 1 and i == chunks - 1:
                token = permute(mark(BRIEF, grad), lambda s, d, t: (s + 1, d, t), range(half - 1, sections - 1))
                gathered.append((high, gather(join(high, where, own_rows, token), high)))
                pinned = (*pinned, token)
            keep, near, own = rest_products(active, where, grad, weights, pinned)
            sums = [
                permute(own.reshape(grad.shape), lambda s, d, t: (s - 1, d, t), [active]),
                permute(near.reshape(grad.shape), lambda s, d, t: (s - 1, d, t ^ 1), [active]),
            ]
            stop = (mark(LONG, keep, before[2]),) if i and not turn else (near,)
            part = add_received(active, where, keep, received, stop)
            sums.append(permute(part.reshape(grad.shape), lambda s, d, t: (s - 1, d, t ^ 2), [active]))
            ended = (part,)
            outgoing.append(sums)
            grads.append(grad)
        incoming = outgoing
        kept.append(grads)

    def send_back(owners, after):
        blocks = cut_shards(where, [(s, kept[sections - 1 - s]) for s in owners], after)
        return [permute(block, lambda s, d, t: (s + 1, d, t ^ k), owners) for k, block in enumerate(blocks)]

    first_products, finals, last_grads = [], [], []
    picked = pick(where, [(s, kept[sections - 1 - s]) for s in high], ended)
    others = swap(picked, high)
    ended = (*ended, *gathered[-1][1][1:3], *others)
    for i in range(chunks):
        grad, near, keep, lead, own = last_products(0, where, incoming[i], weights, ended)
        first_products.append((keep, permute(lead, across(1), [0])))
        finals.append([own, permute(near, across(1), [0])])
        swapped.append(swap(grad, [0]))
        if not i:
            picked = pick(where, [(s, kept[sections - 1 - s]) for s in low[1:]], (grad,))
            others = swap(picked, low[1:]) + others
            ended = (mark(LONG, keep, *incoming[-1]),)
        last_grads.append(grad)
    kept.append(last_grads)
    ended = (keep,)
    for i, (keep, received) in enumerate(first_products):
        if i:
            ended = (mark(LONG, *ended, received, finals[0][1], *swapped[0], *others[:replicas - 1]),)
        part = add_received(0, where, keep, received, ended)
        finals[i].append(permute(part, across(2), [0]))
        ended = (part,)

    back = send_back(range(sections - 1), (part, finals[-1][1], *swapped[-1]))
    weight_grad = weight_products(where, gathered, half, kept[::-1], list(zip(*swapped)), others)
    own_input = place_inputs(where, first_inputs(where, finals, tokens, model, weight_grad), back)
    return (own_input[None], weight_grad[None])


def solution(mesh):
    placed = (
        P("section", ("dp", "tensor"), None),
        P("section", None, "tensor"),
        P(("dp", "tensor"), None),
    )
    sizes = [mesh.shape[a] for a in AXES]
    return jax.shard_map(
        functools.partial(on_device, *sizes),
        mesh=mesh,
        in_specs=placed,
        out_specs=(P("section", ("dp", "tensor"), None), P("section", "dp", "tensor")),
        check_vma=False,
    )
```

```python
import functools

import jax
import jax.numpy as jnp
from jax import lax
from jax.experimental import pallas as pl
from jax.experimental.pallas import tpu as pltpu
from jax.sharding import PartitionSpec as P

AXES = ("section", "dp", "tensor")
CHUNKS = 2
VMEM = 56 * 1024 * 1024
ADD = 56 * 1024 * 1024
SMALL = 56 * 1024 * 1024
TAIL = 48 * 1024 * 1024
F32 = jnp.float32
BF16 = jnp.bfloat16
LONG = pl.CostEstimate(flops=200000000000, bytes_accessed=1000, transcendentals=0)
BRIEF = pl.CostEstimate(flops=1000, bytes_accessed=1000, transcendentals=0)
ANY = pl.BlockSpec(memory_space=pl.ANY)


def params(limit=VMEM):
    return pltpu.CompilerParams(vmem_limit_bytes=limit)


def divisor(total, options):
    for option in options:
        if total % option == 0:
            return option
    return total


def product(lhs, rhs):
    return lax.dot_general(lhs, rhs, (((1,), (1,)), ((), ())), preferred_element_type=F32)


def products_kernel(active, order, count, after, formed, where_ref, *refs):
    parts, weight_ref, outs = refs[:count], refs[count], refs[count + 1 + after:-6]
    part_mem, grad_mem, weight_mem, out_mem, load_sem, store_sem = refs[-6:]
    rows, width = grad_mem.shape[0] * grad_mem.shape[1], grad_mem.shape[2]

    @pl.when(where_ref[1] == active)
    def _():
        part_loads = [
            pltpu.make_async_copy(part, part_mem.at[p], load_sem.at[p]) for p, part in enumerate(parts)
        ]
        weight_loads = [
            pltpu.make_async_copy(weight_ref.at[where_ref[0] ^ k], weight_mem.at[b], load_sem.at[count + b])
            for b, k in enumerate(order)
        ]
        for load in part_loads + weight_loads:
            load.start()
        for load in part_loads:
            load.wait()
        if formed:
            total = part_mem[0].astype(F32)
            for p in range(1, count):
                total = total + part_mem[p].astype(F32)
            grad_mem[...] = total.astype(BF16)
            source = grad_mem
        else:
            source = part_mem.at[0]
        stores = []
        if formed:
            stores.append(pltpu.make_async_copy(grad_mem, outs[0], store_sem.at[0]))
            stores[0].start()
        first = len(stores)
        blocks = [
            pltpu.make_async_copy(out_mem.at[b], outs[first + b], store_sem.at[first + b]) for b in range(len(order))
        ]

        @pl.loop(0, len(order))
        def _(b):
            pltpu.make_async_copy(weight_mem.at[b], weight_mem.at[b], load_sem.at[count + b]).wait()
            total = product(source[...].reshape(rows, width), weight_mem[b])

            @pl.when(order[0] - b != 0)
            def _():
                out_mem[b] = total.astype(BF16)

            @pl.when(order[0] - b == 0)
            def _():
                out_mem[b] = (total + source[...].reshape(rows, width).astype(F32)).astype(BF16)

            for n, block in enumerate(blocks):
                @pl.when(b == n)
                def _():
                    block.start()

        stores.extend(blocks)
        for store in stores:
            store.wait()


def products(active, where, parts, weights, order, formed, name, cost, after=()):
    shards, width, _ = weights.shape
    shape = parts[0].shape
    tokens = shape[0] * shape[1]
    loads = len(parts) + len(order)
    block = jax.ShapeDtypeStruct((tokens, width), BF16)
    return pl.pallas_call(
        functools.partial(products_kernel, active, order, len(parts), len(after), formed),
        in_specs=[pl.BlockSpec(memory_space=pltpu.SMEM)] + [ANY] * (len(parts) + 1 + len(after)),
        out_specs=[ANY] * (len(order) + formed),
        out_shape=[jax.ShapeDtypeStruct(shape, BF16)] * formed + [block] * len(order),
        scratch_shapes=[
            pltpu.VMEM((len(parts), *shape), BF16),
            pltpu.VMEM(shape, BF16),
            pltpu.VMEM((len(order), width, width), BF16),
            pltpu.VMEM((len(order), tokens, width), BF16),
            pltpu.SemaphoreType.DMA((loads,)),
            pltpu.SemaphoreType.DMA((len(order) + formed,)),
        ],
        compiler_params=params(),
        cost_estimate=cost,
        name=name,
    )(where, *parts, weights, *after)


def lead_products(active, where, parts, weights, after=()):
    return products(active, where, parts, weights, (3,), 1, "lead_products", BRIEF, after)


def rest_products(active, where, grad, weights, after=()):
    return products(active, where, (grad,), weights, (2, 1, 0), 0, "rest_products", LONG, after)


def add_kernel(active, where_ref, kept_ref, received_ref, *refs):
    out_ref, kept, received, total, sem = refs[-5:]

    @pl.when(where_ref[1] == active)
    def _():
        loads = [
            pltpu.make_async_copy(kept_ref, kept, sem.at[0]),
            pltpu.make_async_copy(received_ref, received, sem.at[1]),
        ]
        for load in loads:
            load.start()
        for load in loads:
            load.wait()
        total[...] = (kept[...].astype(F32) + received[...].astype(F32)).astype(BF16)
        store = pltpu.make_async_copy(total, out_ref, sem.at[2])
        store.start()
        store.wait()


def add_received(active, where, kept, received, after=()):
    return pl.pallas_call(
        functools.partial(add_kernel, active),
        in_specs=[pl.BlockSpec(memory_space=pltpu.SMEM)] + [ANY] * (2 + len(after)),
        out_specs=ANY,
        out_shape=jax.ShapeDtypeStruct(received.shape, BF16),
        scratch_shapes=[pltpu.VMEM(received.shape, BF16)] * 3 + [pltpu.SemaphoreType.DMA((3,))],
        compiler_params=params(ADD),
        cost_estimate=BRIEF,
        name="add_received",
    )(where, kept, received, *after)


def last_kernel(active, count, after, where_ref, *refs):
    parts, weight_ref, outs = refs[:count], refs[count], refs[count + 1 + after:-7]
    part_mem, grad_mem, weight_mem, out_mem, own_mem, load_sem, store_sem = refs[-7:]
    shards, rows, width = grad_mem.shape

    @pl.when(where_ref[1] == active)
    def _():
        part_loads = [
            pltpu.make_async_copy(part, part_mem.at[p], load_sem.at[p]) for p, part in enumerate(parts)
        ]
        weight_loads = [
            pltpu.make_async_copy(weight_ref.at[n], weight_mem.at[n], load_sem.at[count + n]) for n in range(shards)
        ]
        for load in part_loads + weight_loads:
            load.start()
        for load in part_loads:
            load.wait()
        total = part_mem[0].astype(F32)
        for p in range(1, count):
            total = total + part_mem[p].astype(F32)
        part_mem[0] = total.astype(BF16)
        stores = [pltpu.make_async_copy(part_mem.at[0], outs[0], store_sem.at[0])]
        stores[0].start()
        for k in range(shards):
            grad_mem[k] = part_mem[0, where_ref[0] ^ k]

        @pl.loop(0, shards)
        def _(n):
            pltpu.make_async_copy(weight_mem.at[n], weight_mem.at[n], load_sem.at[count + n]).wait()
            at = pl.ds(pl.multiple_of(n * width, 128), width)
            total = product(grad_mem[...].reshape(shards * rows, width), weight_mem[n])
            through = grad_mem[...].reshape(shards * rows, width).astype(F32)
            total = total + jnp.where(where_ref[0] == n, through, 0.0)
            own_mem[:, at] = total[:rows]
            for k in range(1, shards):
                out_mem[k - 1, :, at] = total[k * rows:(k + 1) * rows].astype(BF16)

        for k in range(1, shards):
            stores.append(pltpu.make_async_copy(out_mem.at[k - 1], outs[k], store_sem.at[k]))
        stores.append(pltpu.make_async_copy(own_mem, outs[shards], store_sem.at[shards]))
        for store in stores[1:]:
            store.start()
        for store in stores:
            store.wait()


def last_products(active, where, parts, weights, after=()):
    shards, width, _ = weights.shape
    shape = parts[0].shape
    rows = shape[1]
    half = jax.ShapeDtypeStruct((rows, shards * width), BF16)
    return pl.pallas_call(
        functools.partial(last_kernel, active, len(parts), len(after)),
        in_specs=[pl.BlockSpec(memory_space=pltpu.SMEM)] + [ANY] * (len(parts) + 1 + len(after)),
        out_specs=[ANY] * (shards + 1),
        out_shape=[jax.ShapeDtypeStruct(shape, BF16)]
        + [half] * (shards - 1)
        + [jax.ShapeDtypeStruct((rows, shards * width), F32)],
        scratch_shapes=[
            pltpu.VMEM((len(parts), *shape), BF16),
            pltpu.VMEM(shape, BF16),
            pltpu.VMEM(weights.shape, BF16),
            pltpu.VMEM((shards - 1, rows, shards * width), BF16),
            pltpu.VMEM((rows, shards * width), F32),
            pltpu.SemaphoreType.DMA((len(parts) + shards,)),
            pltpu.SemaphoreType.DMA((shards + 1,)),
        ],
        compiler_params=params(),
        cost_estimate=BRIEF,
        name="last_products",
    )(where, *parts, weights, *after)


def place_kernel(count, where_ref, *refs):
    pieces, outs = refs[:count], refs[count:]
    rows = outs[0].shape[1]
    for i, out_ref in enumerate(outs):
        for k, piece in enumerate(pieces):
            out_ref[where_ref[0] ^ k] = piece[i * rows:(i + 1) * rows]


def place_shards(where, pieces, chunks):
    tokens, width = pieces[0].shape
    memory = pl.BlockSpec(memory_space=pltpu.VMEM)
    return pl.pallas_call(
        functools.partial(place_kernel, len(pieces)),
        in_specs=[pl.BlockSpec(memory_space=pltpu.SMEM)] + [memory] * len(pieces),
        out_specs=[memory] * chunks,
        out_shape=[jax.ShapeDtypeStruct((len(pieces), tokens // chunks, width), BF16)] * chunks,
        compiler_params=params(SMALL),
        name="place_shards",
    )(where, *pieces)


def first_kernel(where_ref, *refs):
    out_ref = refs[-1]
    for i in range((len(refs) - 2) // 3):
        own, near, far = refs[3 * i:3 * i + 3]
        rows = own.shape[0]
        total = (own[...] + near[...].astype(F32) + far[...].astype(F32)).astype(BF16)
        out_ref[i * rows:(i + 1) * rows] = jnp.where(where_ref[1] == 0, total, jnp.zeros_like(total))


def first_inputs(where, sums, tokens, model, after):
    memory = pl.BlockSpec(memory_space=pltpu.VMEM)
    terms = [term for chunk in sums for term in chunk]
    return pl.pallas_call(
        first_kernel,
        in_specs=[pl.BlockSpec(memory_space=pltpu.SMEM)] + [memory] * len(terms) + [ANY],
        out_specs=memory,
        out_shape=jax.ShapeDtypeStruct((tokens, model), BF16),
        compiler_params=params(TAIL),
        cost_estimate=BRIEF,
        name="first_inputs",
    )(where, *terms, after)


def inputs_kernel(where_ref, sums_ref, *refs):
    pieces, out_ref = refs[:-1], refs[-1]
    width = pieces[0].shape[-1]
    for k, piece in enumerate(pieces):
        columns = pl.ds(pl.multiple_of((where_ref[0] ^ k) * width, 128), width)
        out_ref[:, columns] = sums_ref[:, columns] + piece[...]


def place_inputs(where, sums, pieces):
    memory = pl.BlockSpec(memory_space=pltpu.VMEM)
    return pl.pallas_call(
        inputs_kernel,
        in_specs=[pl.BlockSpec(memory_space=pltpu.SMEM)] + [memory] * (1 + len(pieces)),
        out_specs=memory,
        out_shape=jax.ShapeDtypeStruct(sums.shape, BF16),
        compiler_params=params(TAIL),
        name="place_inputs",
    )(where, sums, *pieces)


def cut_kernel(owners, chunks, where_ref, *refs):
    held, sem = refs[-2:]
    shards = held.shape[0]
    outs = refs[-2 - shards:-2]
    rows = refs[0].shape[1]
    for o, section in enumerate(owners):
        grads = refs[o * chunks:(o + 1) * chunks]

        @pl.when(where_ref[1] == section)
        def _():
            loads = [
                pltpu.make_async_copy(grad.at[where_ref[0] ^ k], held.at[k, pl.ds(i * rows, rows)], sem.at[k, i])
                for k in range(shards)
                for i, grad in enumerate(grads)
            ]
            for load in loads:
                load.start()
            for load in loads:
                load.wait()
            stores = [pltpu.make_async_copy(held.at[k], out, sem.at[k, 0]) for k, out in enumerate(outs)]
            for store in stores:
                store.start()
            for store in stores:
                store.wait()


def cut_shards(where, owners, after):
    grads = [grad for _, chunk in owners for grad in chunk]
    chunks = len(owners[0][1])
    shards, rows, width = grads[0].shape
    tokens = rows * chunks
    return pl.pallas_call(
        functools.partial(cut_kernel, [section for section, _ in owners], chunks),
        in_specs=[pl.BlockSpec(memory_space=pltpu.SMEM)] + [ANY] * (len(grads) + len(after)),
        out_specs=[ANY] * shards,
        out_shape=[jax.ShapeDtypeStruct((tokens, width), BF16)] * shards,
        scratch_shapes=[
            pltpu.VMEM((shards, tokens, width), BF16),
            pltpu.SemaphoreType.DMA((shards, chunks)),
        ],
        compiler_params=params(SMALL),
        cost_estimate=BRIEF,
        name="cut_shards",
    )(where, *grads, *after)


def pick_kernel(owners, chunks, where_ref, *refs):
    out_ref, held, sem = refs[-3:]
    for o, section in enumerate(owners):
        grads = refs[o * chunks:(o + 1) * chunks]

        @pl.when(where_ref[1] == section)
        def _():
            loads = [pltpu.make_async_copy(grad, held.at[i], sem.at[i]) for i, grad in enumerate(grads)]
            for load in loads:
                load.start()
            for load in loads:
                load.wait()
            store = pltpu.make_async_copy(held, out_ref, sem.at[0])
            store.start()
            store.wait()


def pick(where, owners, after):
    grads = [grad for _, chunk in owners for grad in chunk]
    shape = (len(owners[0][1]), *grads[0].shape)
    return pl.pallas_call(
        functools.partial(pick_kernel, [section for section, _ in owners], shape[0]),
        in_specs=[pl.BlockSpec(memory_space=pltpu.SMEM)] + [ANY] * (len(grads) + len(after)),
        out_specs=ANY,
        out_shape=jax.ShapeDtypeStruct(shape, BF16),
        scratch_shapes=[pltpu.VMEM(shape, BF16), pltpu.SemaphoreType.DMA(shape[:1])],
        compiler_params=params(SMALL),
        cost_estimate=BRIEF,
        name="pick",
    )(where, *grads, *after)


def mark_kernel(*refs):
    refs[-1][...] = jnp.zeros_like(refs[-1])


def mark(cost, *after):
    return pl.pallas_call(
        mark_kernel,
        in_specs=[ANY] * len(after),
        out_specs=pl.BlockSpec(memory_space=pltpu.VMEM),
        out_shape=jax.ShapeDtypeStruct((8, 128), F32),
        compiler_params=params(SMALL),
        cost_estimate=cost,
        name="mark",
    )(*after)


def join_kernel(sections, count, where_ref, *refs):
    parts, out_ref, held, sem = refs[:count], refs[-3], refs[-2], refs[-1]
    rows = parts[0].shape[0]

    @pl.when((where_ref[1] >= sections[0]) & (where_ref[1] <= sections[-1]))
    def _():
        loads = [
            pltpu.make_async_copy(part, held.at[pl.ds(j * rows, rows)], sem.at[j]) for j, part in enumerate(parts)
        ]
        for load in loads:
            load.start()
        for load in loads:
            load.wait()
        store = pltpu.make_async_copy(held, out_ref, sem.at[0])
        store.start()
        store.wait()


def join(sections, where, parts, after):
    rows, width = parts[0].shape
    return pl.pallas_call(
        functools.partial(join_kernel, sections, len(parts)),
        in_specs=[pl.BlockSpec(memory_space=pltpu.SMEM)] + [ANY] * (len(parts) + 1),
        out_specs=ANY,
        out_shape=jax.ShapeDtypeStruct((rows * len(parts), width), BF16),
        scratch_shapes=[pltpu.VMEM((rows * len(parts), width), BF16), pltpu.SemaphoreType.DMA((len(parts),))],
        compiler_params=params(SMALL),
        cost_estimate=BRIEF,
        name="join",
    )(where, *parts, after)


def weight_kernel(owners, half, sections, shards, replicas, chunks, where_ref, *refs):
    groups, grads = refs[:len(owners) * shards], refs[len(owners) * shards:-6]
    out_ref, saved, ordered, out_mem, load_sem, store_sem = refs[-6:]
    _, rows, width = grads[0].shape
    tokens = chunks * rows
    step = out_mem.shape[1]
    steps = out_ref.shape[0] // step

    loads = []
    for k in range(shards):
        for g, owner in enumerate(owners):
            @pl.when((where_ref[1] >= owner[0]) & (where_ref[1] <= owner[-1]))
            def _():
                pltpu.make_async_copy(groups[g * shards + k], saved.at[k], load_sem.at[k]).start()

        loads.append(pltpu.make_async_copy(groups[k], saved.at[k], load_sem.at[k]))
    def grad_loads(section):
        for k in range(shards):
            for j in range(replicas):
                for i in range(chunks):
                    if j == 0:
                        grad = grads[section * chunks + i]
                    elif section == 0:
                        grad = grads[(sections + j - 1) * chunks + i]
                    else:
                        later = (replicas - 1) * (section >= half)
                        grad = grads[(sections + replicas - 1) * chunks + later + j - 1].at[i]
                    at = (k * replicas + j) * tokens + i * rows
                    yield pltpu.make_async_copy(
                        grad.at[where_ref[0] ^ k],
                        ordered.at[pl.ds(at, rows)],
                        load_sem.at[shards + (k * replicas + j) * chunks + i],
                    )

    for section in range(sections):
        @pl.when(where_ref[1] == section)
        def _():
            for load in grad_loads(section):
                load.start()

    loads.extend(grad_loads(0))
    for load in loads:
        load.wait()

    def store(n):
        slot = lax.rem(n, 2)
        return pltpu.make_async_copy(
            out_mem.at[slot], out_ref.at[pl.ds(pl.multiple_of(n * step, step), step)], store_sem.at[slot]
        )

    @pl.loop(0, steps)
    def _(n):
        @pl.when(n >= 2)
        def _():
            store(n - 2).wait()

        features = pl.ds(pl.multiple_of(n * step, step), step)
        out_mem[lax.rem(n, 2)] = lax.dot_general(
            saved[:, :, features].reshape(ordered.shape[0], step),
            ordered[...],
            (((0,), (0,)), ((), ())),
            preferred_element_type=F32,
        )
        store(n).start()

    for n in range(max(steps - 2, 0), steps):
        store(n).wait()


def weight_products(where, gathered, half, own_grads, first_peers, other_peers):
    owners = tuple(tuple(sections) for sections, _ in gathered)
    groups = [array for _, arrays in gathered for array in arrays]
    shards = len(gathered[0][1])
    tokens, features = groups[0].shape
    sections, replicas = len(own_grads), len(first_peers) + 1
    chunks, width = len(own_grads[0]), own_grads[0][0].shape[-1]
    grads = [grad for chunk in (*own_grads, *first_peers) for grad in chunk] + other_peers
    step = divisor(features, (256, 128))
    return pl.pallas_call(
        functools.partial(weight_kernel, owners, half, sections, shards, replicas, chunks),
        in_specs=[pl.BlockSpec(memory_space=pltpu.SMEM)] + [ANY] * (len(groups) + len(grads)),
        out_specs=ANY,
        out_shape=jax.ShapeDtypeStruct((features, width), F32),
        scratch_shapes=[
            pltpu.VMEM((shards, tokens, features), BF16),
            pltpu.VMEM((shards * tokens, width), BF16),
            pltpu.VMEM((2, step, width), F32),
            pltpu.SemaphoreType.DMA((shards + shards * replicas * chunks,)),
            pltpu.SemaphoreType.DMA((2,)),
        ],
        compiler_params=params(),
        cost_estimate=BRIEF,
        name="weight_products",
    )(where, *groups, *grads)


def on_device(sections, replicas, shards, saved, weight, out_grad):
    tokens, model = out_grad.shape
    width = model // shards
    chunks = CHUNKS
    rows = tokens // chunks
    section, dp, tensor = (lax.axis_index(a) for a in AXES)
    weights = weight[0].reshape(shards, width, width)
    activations = saved[0]

    def place(s, d, t):
        return (s * replicas + d) * shards + t

    def permute(value, route, active):
        pairs = []
        for s in active:
            for d in range(replicas):
                for t in range(shards):
                    to = route(s, d, t)
                    if 0 <= to[0] < sections:
                        pairs.append((place(s, d, t), place(*to)))
        return lax.ppermute(value, AXES, pairs)

    def across(k):
        return lambda s, d, t: (s, d, t ^ k)

    everyone = range(sections)
    where = jnp.stack([tensor, section]).astype(jnp.int32)

    last = sections - 1
    pieces = [lax.dynamic_slice(out_grad, (0, tensor * width), (tokens, width))]
    for k in range(1, shards):
        block = lax.dynamic_slice(out_grad, (0, (tensor ^ k) * width), (tokens, width))
        pieces.append(permute(block, across(k), [last]))
    first = place_shards(where, pieces, chunks)

    height = model // replicas
    own_rows = [lax.dynamic_slice(activations, (0, dp * height), (tokens, height))]
    for j in range(1, replicas):
        block = lax.dynamic_slice(activations, (0, lax.rem(dp + replicas - j, replicas) * height), (tokens, height))
        own_rows.append(
            permute(block, lambda s, d, t: (s, (d - j) % replicas, t), everyone)
        )

    def swap(value, active):
        return [permute(value, lambda s, d, t: (s, (d - j) % replicas, t), active) for j in range(1, replicas)]

    half = sections // 2
    low, high = range(half), range(half, sections)
    def gather(value, active):
        near, far = permute(value, across(1), active), permute(value, across(2), active)
        return [value, near, far, permute(far, across(1), active)]

    gathered, kept = [(low, gather(join(low, where, own_rows, first[0]), low))], []
    swapped = []
    due = {(0, 1): gathered[0][1][1:3], (half, 0): gathered[0][1][3:]}
    incoming = [(first[i],) for i in range(chunks)]
    ended = ()
    for r in range(sections - 1):
        active = sections - 1 - r
        grads, outgoing = [], []
        for i in range(chunks):
            before = outgoing[-1] if i else incoming[-1] if r else ()
            turn = i and active == half - 1
            pinned = (*(before if turn else before[:2]), *due.get((r, i), ()))
            grad, lead = lead_products(active, where, incoming[i], weights, ended)
            received = permute(lead, across(1), [active])
            if active == half - 1 and i == chunks - 1:
                token = permute(mark(BRIEF, grad), lambda s, d, t: (s + 1, d, t), range(half - 1, sections - 1))
                gathered.append((high, gather(join(high, where, own_rows, token), high)))
                pinned = (*pinned, token)
            keep, near, own = rest_products(active, where, grad, weights, pinned)
            sums = [
                permute(own.reshape(grad.shape), lambda s, d, t: (s - 1, d, t), [active]),
                permute(near.reshape(grad.shape), lambda s, d, t: (s - 1, d, t ^ 1), [active]),
            ]
            stop = (mark(LONG, keep, before[2]),) if i and not turn else (near,)
            part = add_received(active, where, keep, received, stop)
            sums.append(permute(part.reshape(grad.shape), lambda s, d, t: (s - 1, d, t ^ 2), [active]))
            ended = (part,)
            outgoing.append(sums)
            grads.append(grad)
        incoming = outgoing
        kept.append(grads)

    def send_back(owners, after):
        blocks = cut_shards(where, [(s, kept[sections - 1 - s]) for s in owners], after)
        return [permute(block, lambda s, d, t: (s + 1, d, t ^ k), owners) for k, block in enumerate(blocks)]

    first_products, finals, last_grads = [], [], []
    picked = pick(where, [(s, kept[sections - 1 - s]) for s in high], ended)
    others = swap(picked, high)
    ended = (*ended, *gathered[-1][1][1:3], *others)
    for i in range(chunks):
        grad, near, keep, lead, own = last_products(0, where, incoming[i], weights, ended)
        first_products.append((keep, permute(lead, across(1), [0])))
        finals.append([own, permute(near, across(1), [0])])
        swapped.append(swap(grad, [0]))
        if not i:
            picked = pick(where, [(s, kept[sections - 1 - s]) for s in low[1:]], (grad,))
            others = swap(picked, low[1:]) + others
            ended = (mark(LONG, keep, *incoming[-1]),)
        last_grads.append(grad)
    kept.append(last_grads)
    ended = (keep,)
    for i, (keep, received) in enumerate(first_products):
        if i:
            ended = (mark(LONG, *ended, received, finals[0][1], *swapped[0], *others[:replicas - 1]),)
        part = add_received(0, where, keep, received, ended)
        finals[i].append(permute(part, across(2), [0]))
        ended = (part,)

    back = send_back(range(sections - 1), (part, finals[-1][1], *swapped[-1]))
    weight_grad = weight_products(where, gathered, half, kept[::-1], list(zip(*swapped)), others)
    own_input = place_inputs(where, first_inputs(where, finals, tokens, model, weight_grad), back)
    return (own_input[None], weight_grad[None])


def solution(mesh):
    placed = (
        P("section", ("dp", "tensor"), None),
        P("section", None, "tensor"),
        P(("dp", "tensor"), None),
    )
    sizes = [mesh.shape[a] for a in AXES]
    return jax.shard_map(
        functools.partial(on_device, *sizes),
        mesh=mesh,
        in_specs=placed,
        out_specs=(P("section", ("dp", "tensor"), None), P("section", "dp", "tensor")),
        check_vma=False,
    )
```
